32 devices in a mesh: row: 8 (over y, x, core), col: 4 (over z).
Axes of the slice: x: 2, y: 2, z: 4, core: 2. Of those that a mesh axis runs over, the one named last changes fastest.
Arguments:
- density_blocks: float32 [96, 6, 256, 256], P(('row', 'col')), may hold values from -5 to 5
- density_live: int32 [96, 6], P(('row', 'col')), may hold values 0 or 1
- tangent_blocks: float32 [96, 6, 256, 256], P(('row', 'col')), may hold values from -1.5 to 1.5
- tangent_live: int32 [96, 6], P(('row', 'col')), may hold values 0 or 1
- block_offsets: int32 [96, 6], P(('row', 'col')), may hold values from -3 to 3, as said below
Outputs:
- tangent_next: float32 [96, 6, 256, 256], P(('row', 'col'))
- mean_trace: float32 [], replicated
The draws below stay inside these ranges and needn't reach their ends.
Inputs may be any that keep to these rules, and one draw needn't show every extreme that they name: `block_offsets`: within each block row the 6 offsets are distinct and ascending.
All inputs are finite; a program needn't handle non-finite values. No bound on the sum of `density_live` or of `tangent_live` on one device may be relied on, other than what follows from the above.
Results may differ from the reference program's by a relative error of at most 0.0003.
Values sent between devices are 32-bit elements; how exact they have to be, the bound alone decides.
No kernel may reach another device: no remote copies, remote signals or barrier semaphores. Data moves between devices by JAX's collectives and lax.ppermute only.
A program may use at most 384 MiB of HBM per device.

```python
import jax
import jax.numpy as jnp
from jax import lax

BLOCK = 256
HALF = 3
SLOTS = 6
BLOCK_ROWS = 96


def draw_block_offsets(key, part):
    width = 2 * HALF + 1
    scores = jax.random.randint(key, (BLOCK_ROWS, width), 0, 1 << 20) * width + jnp.arange(width, dtype=jnp.int32)[None, :]
    chosen = lax.top_k(scores, SLOTS)[1]
    return (jnp.sort(chosen, axis=1) - HALF).astype(jnp.int32)


def draw_density_blocks(key, part):
    height = jnp.arange(BLOCK_ROWS, dtype=jnp.float32) / (BLOCK_ROWS - 1)
    values = jax.random.truncated_normal(key, -6.0, 6.0, (BLOCK_ROWS, SLOTS, BLOCK, BLOCK), jnp.float32)
    scales = (1.0 + 2.0 * height) / jnp.sqrt(float(BLOCK))
    return (values * scales[:, None, None, None]).astype(jnp.float32)


def with_ends(array, key, least, top_value):
    index_at = [jax.random.randint(jax.random.fold_in(key, axis), (), 0, length) for axis, length in enumerate(array.shape)]
    widest = array.shape.index(max(array.shape))
    beside = index_at[:widest] + [(index_at[widest] + 1) % array.shape[widest]] + index_at[widest + 1:]
    return array.at[tuple(index_at)].set(least).at[tuple(beside)].set(top_value)


def levels(key, shape, cuts, least, top_value):
    loudness = 1.0
    for dim, shards_of in cuts:
        steps = jax.random.uniform(jax.random.fold_in(jax.random.fold_in(key, 6), dim), (shards_of,), jnp.float32, least / len(cuts), top_value / len(cuts))
        loudness = loudness * jnp.repeat(jnp.exp(steps), shape[dim] // shards_of).reshape((-1,) + (1,) * (len(shape) - 1 - dim))
    return loudness


def noise(rng, dims, scale, most, shards=(), kind=jnp.bfloat16):
    values = scale * jax.random.normal(rng, dims, jnp.float32)
    if shards:
        values = values * levels(rng, dims, shards, -0.22, 0.18)
    return jnp.clip(values, -most, most).astype(kind)


def setup_inputs(seed: int = 0) -> dict:
    splits = jax.random.split(jax.random.key(seed), 6)
    density_blocks = draw_density_blocks(jax.random.fold_in(splits[5], 71), 0)
    density_live = with_ends((jax.random.randint(splits[1], (BLOCK_ROWS, SLOTS), 0, 3) < 2).astype(jnp.int32), jax.random.fold_in(splits[1], 1), 0, 1)
    tangent_blocks = noise(splits[2], (BLOCK_ROWS, SLOTS, BLOCK, BLOCK), 0.25, 1.5, ((0, 32),), jnp.float32)
    tangent_live = with_ends((jax.random.randint(splits[3], (BLOCK_ROWS, SLOTS), 0, 3) < 2).astype(jnp.int32), jax.random.fold_in(splits[3], 1), 0, 1)
    block_offsets = draw_block_offsets(jax.random.fold_in(splits[5], 71), 0)
    return dict(density_blocks=density_blocks, density_live=density_live, tangent_blocks=tangent_blocks, tangent_live=tangent_live, block_offsets=block_offsets)


def band_layout(values, live, offsets):
    width = 2 * HALF + 1
    places = jnp.arange(width, dtype=jnp.int32) - HALF
    select = ((offsets[:, :, None] == places[None, None, :]) & (live[:, :, None] == 1)).astype(values.dtype)
    return jnp.einsum("rsp,rsab->rpab", select, values, precision=lax.Precision.HIGHEST)


def band_product(stacked, count):
    width = 2 * HALF + 1
    result = jnp.zeros((count, width, stacked.shape[-2], stacked.shape[-1]), stacked.dtype)
    for shift_value in range(-HALF, HALF + 1):
        low_place = max(0, shift_value)
        high_place = min(2 * HALF, shift_value + 2 * HALF)
        left_blocks = stacked[HALF:HALF + count, :, shift_value + HALF]
        right_blocks = stacked[HALF + shift_value:HALF + shift_value + count, ::-1, low_place - shift_value:high_place - shift_value + 1]
        partial_sum = jnp.einsum("rkab,rknbc->rnac", left_blocks, right_blocks, precision=lax.Precision.HIGHEST)
        result = result.at[:, low_place:high_place + 1].add(partial_sum)
    return result


def reference(density_blocks, density_live, tangent_blocks, tangent_live, block_offsets):
    total = density_blocks.shape[0]

    def one_row(center):
        nearby = (center + jnp.arange(-HALF, HALF + 1, dtype=jnp.int32)) % total
        nearby = nearby.astype(jnp.int32)
        first_band = band_layout(density_blocks[nearby], density_live[nearby], block_offsets[nearby])
        second_band = band_layout(tangent_blocks[nearby], tangent_live[nearby], block_offsets[nearby])
        stacked = jnp.stack([first_band, second_band], axis=1)
        product = band_product(stacked, 1)[0]
        chosen = product[block_offsets[center] + HALF]
        weights = tangent_live[center].astype(density_blocks.dtype)
        combined = 1.5 * weights[:, None, None] * tangent_blocks[center] - 0.5 * chosen
        return combined, jnp.trace(product[HALF])

    tangent_next, traces = lax.map(one_row, jnp.arange(total, dtype=jnp.int32))
    return tangent_next, jnp.sum(traces) / total
```

```python
import functools

import jax
import jax.numpy as jnp
from jax import lax
from jax.experimental import pallas as pl
from jax.experimental.pallas import tpu as pltpu
from jax.sharding import PartitionSpec as P

HALF = 3
WIDTH = 2 * HALF + 1
WIN = 2 * HALF
AXES = ("row", "col")
VMEM_LIMIT = 58 * 1024 * 1024
F32 = jnp.float32
BF16 = jnp.bfloat16
I32 = jnp.int32


def need_cells(side):
    base = 0 if side == 0 else HALF
    return [
        (t, k, j)
        for t in range(2)
        for k in range(HALF)
        for j in range(WIN)
        if abs(j - (base + k)) <= HALF
    ]


def cell(t, k, j):
    return (t * HALF + k) * WIN + j


CELLS = 2 * HALF * WIN
COUNT_ROW = 2 * CELLS
PLAN_ROWS = 2 * CELLS + 8


def plan_kernel(slots, me_ref, meta_ref, out_ref, table):
    n = meta_ref.shape[-1]
    fields = 3 * slots

    def row(i, f):
        source, r = (0, i) if i < HALF else (1, i - HALF)
        at = r * fields + f
        return meta_ref[source, at : at + 1, :]

    one = jnp.ones((1, n), I32)
    zero = jnp.zeros((1, n), I32)
    live = [{}, {}]
    stored = {}
    for i in range(WIN):
        offs = [row(i, 2 * slots + s) for s in range(slots)]
        flags = [[jnp.where(row(i, t * slots + s) == 1, one, zero) for s in range(slots)] for t in range(2)]
        for j in range(WIN):
            d = j - i
            if abs(d) > HALF:
                continue
            here = [jnp.where(o == d, one, zero) for o in offs]
            stored[i, j] = one if d == 0 else functools.reduce(jnp.bitwise_or, here)
            for t in range(2):
                live[t][i, j] = functools.reduce(jnp.bitwise_or, [h & f for h, f in zip(here, flags[t])])

    table[...] = jnp.full(table.shape, -1, I32)
    most = zero
    for side in range(2):
        base, other = (0, HALF) if side == 0 else (HALF, 0)
        count = zero
        for t, k, j in need_cells(side):
            kk = base + k
            users = [
                live[1 - t][i, kk] & stored[i, j]
                for i in range(other, other + HALF)
                if abs(i - kk) <= HALF and abs(j - i) <= HALF
            ]
            need = functools.reduce(jnp.bitwise_or, users) & live[t][kk, j]
            at = side * CELLS + cell(t, k, j)
            table[at : at + 1, :] = jnp.where(need == 1, count, -one)
            count = count + need
        table[COUNT_ROW + side : COUNT_ROW + side + 1, :] = count
        most = jnp.maximum(most, count)
    top = jnp.max(most.astype(F32), axis=1, keepdims=True).astype(I32)
    table[COUNT_ROW + 2 : COUNT_ROW + 3, :] = jnp.broadcast_to(top, (1, n))

    me = me_ref[0]
    whole = table[...]
    lane = lax.broadcasted_iota(I32, whole.shape, 1)
    right = lax.rem(me + 1, n)
    first = jnp.sum(jnp.where(lane == me, whole, 0), axis=1, keepdims=True)
    second = jnp.sum(jnp.where(lane == right, whole, 0), axis=1, keepdims=True)
    out_lane = lax.broadcasted_iota(I32, out_ref.shape, 1)
    out_ref[...] = jnp.where(out_lane == 0, first, second)


def make_plan(meta, me, slots):
    n, rows = meta.shape[0], meta.shape[1]
    low = jnp.roll(meta[:, rows - HALF :], 1, axis=0).reshape(n, -1).T
    high = meta[:, :HALF].reshape(n, -1).T
    return pl.pallas_call(
        functools.partial(plan_kernel, slots),
        out_shape=jax.ShapeDtypeStruct((PLAN_ROWS, 128), I32),
        in_specs=[pl.BlockSpec(memory_space=pltpu.SMEM), pl.BlockSpec(memory_space=pltpu.VMEM)],
        out_specs=pl.BlockSpec(memory_space=pltpu.VMEM),
        scratch_shapes=[pltpu.VMEM((PLAN_ROWS, n), I32)],
        name="plan",
    )(me.reshape(1), jnp.stack([low, high]))


def pack_kernel(rows, own_ref, forth_ref, back_ref, x_ref, t_ref, forth_out, back_out, sems):
    stored = x_ref.shape[0]

    def each(act):
        index = 0
        for side, at_ref, out in ((0, forth_ref, forth_out), (1, back_ref, back_out)):
            for t, k, j in need_cells(side):
                own_row = rows - HALF + k if side == 0 else k
                place = j - k + HALF if side == 0 else j - k
                at = at_ref[cell(t, k, j)]
                source = (x_ref, t_ref)[t]
                sem = sems.at[index]
                index += 1

                @pl.when(at >= 0)
                def _():
                    block = own_ref[(t * rows + own_row) * WIDTH + place] - t * stored
                    act(pltpu.make_async_copy(source.at[block], out.at[at], sem))

    each(lambda copy: copy.start())
    each(lambda copy: copy.wait())


def pack(own, forth, back, x, t, room, rows):
    smem = pl.BlockSpec(memory_space=pltpu.SMEM)
    hbm = pl.BlockSpec(memory_space=pl.ANY)
    shape = jax.ShapeDtypeStruct((room,) + x.shape[1:], F32)
    return pl.pallas_call(
        functools.partial(pack_kernel, rows),
        out_shape=(shape, shape),
        in_specs=[smem, smem, smem, hbm, hbm],
        out_specs=(hbm, hbm),
        scratch_shapes=[pltpu.SemaphoreType.DMA((2 * len(need_cells(0)),))],
        name="pack",
    )(own, forth, back, x, t)


def halves(values):
    high = values.astype(BF16)
    return high, (values - high.astype(F32)).astype(BF16)


def product(lh, ll, rh, rl):
    dot = functools.partial(jnp.dot, preferred_element_type=F32)
    return dot(lh, rh) + (dot(lh, rl) + dot(ll, rh))


def own_kernel(
    rows, slots, room,
    own_ref, left_ref, right_ref, off_ref, x_ref, t_ref,
    part_ref, high_ref, low_ref, lists_ref,
    local_ref,
):
    stored = rows * slots
    outs = stored + rows

    def split(i, carry):
        for t, source in enumerate((x_ref, t_ref)):
            high, low = halves(source[i])
            high_ref[t * stored + i] = high
            low_ref[t * stored + i] = low
        return carry

    lax.fori_loop(0, stored, split, 0)

    def of_output(q, counts):
        is_diag = q >= stored
        row = jnp.where(is_diag, q - stored, lax.div(q, slots))
        d = jnp.where(is_diag, 0, off_ref[jnp.minimum(q, stored - 1)])
        has_zero = jnp.bool_(False)
        for s in range(slots):
            has_zero = has_zero | (off_ref[row * slots + s] == 0)
        wanted = jnp.logical_not(is_diag & has_zero)
        lists_ref[2, q] = counts[1]
        local_ref[2, q] = counts[0]

        def of_term(m, counts):
            t = lax.rem(m, 2)
            e = lax.div(m, 2) - HALF
            k = row + e
            place = d - e + HALF
            ok = wanted & (place >= 0) & (place < WIDTH)
            left = own_ref[(t * rows + row) * WIDTH + e + HALF]
            ok = ok & (left >= 0)
            column = row + d
            own_side = (k >= 0) & (k < rows)
            own_at = jnp.where(ok & own_side, ((1 - t) * rows + k) * WIDTH + place, 0)
            own_block = own_ref[own_at]
            low_at = jnp.where(ok & (k < 0), ((1 - t) * HALF + k + HALF) * WIN + column + HALF, 0)
            low_block = left_ref[low_at]
            high_at = jnp.where(
                ok & (k >= rows), ((1 - t) * HALF + k - rows) * WIN + column - rows + HALF, 0
            )
            high_block = right_ref[high_at]
            far_block = jnp.where(k < 0, low_block, high_block)
            far_place = jnp.where(k < 0, low_block, high_block + room)
            near, far = counts
            local_ref[0, near] = left
            local_ref[1, near] = own_block
            near = near + jnp.where(ok & own_side & (own_block >= 0), 1, 0)
            lists_ref[0, far] = left
            lists_ref[1, far] = far_place
            far = far + jnp.where(ok & jnp.logical_not(own_side) & (far_block >= 0), 1, 0)
            return near, far

        return lax.fori_loop(0, 2 * WIDTH, of_term, counts)

    near, far = lax.fori_loop(0, outs, of_output, (jnp.int32(0), jnp.int32(0)))
    lists_ref[2, outs] = far
    local_ref[2, outs] = near

    def compute(q, carry):
        part_ref[q] = jnp.zeros(part_ref.shape[1:], F32)

        def term(m, carry):
            left = local_ref[0, m]
            right = local_ref[1, m]
            part_ref[q] += product(high_ref[left], low_ref[left], high_ref[right], low_ref[right])
            return carry

        return lax.fori_loop(local_ref[2, q], local_ref[2, q + 1], term, carry)

    lax.fori_loop(0, outs, compute, 0)


def list_length(rows, slots):
    return -(-((rows * slots + rows) * 2 * WIDTH + 1) // 128) * 128


def own_part(own, left, right, offsets, x, t, room, rows, slots):
    smem = pl.BlockSpec(memory_space=pltpu.SMEM)
    vmem = pl.BlockSpec(memory_space=pltpu.VMEM)
    stored = rows * slots
    block = x.shape[1:]
    length = list_length(rows, slots)
    return pl.pallas_call(
        functools.partial(own_kernel, rows, slots, room),
        out_shape=(
            jax.ShapeDtypeStruct((stored + rows,) + block, F32),
            jax.ShapeDtypeStruct((2 * stored,) + block, BF16),
            jax.ShapeDtypeStruct((2 * stored,) + block, BF16),
            jax.ShapeDtypeStruct((3, length), I32),
        ),
        in_specs=[smem, smem, smem, smem, vmem, vmem],
        out_specs=(vmem, vmem, vmem, smem),
        scratch_shapes=[pltpu.SMEM((3, length), I32)],
        compiler_params=pltpu.CompilerParams(vmem_limit_bytes=VMEM_LIMIT),
        cost_estimate=pl.CostEstimate(
            flops=60 * 3 * 2 * block[0] ** 3, bytes_accessed=30 * 2**20, transcendentals=0
        ),
        name="own_rows",
    )(own, left, right, offsets, x, t)


def halo_kernel(
    rows, slots, room,
    lists_ref, counts_ref, off_ref, weight_ref,
    low_ref, high_ref, own_high_ref, own_low_ref, part_ref, t_ref,
    out_ref, trace_ref,
    stage, far_high, far_low, own_high, own_low, total, tangent, stage_sems, sems,
):
    stored = rows * slots
    outs = stored + rows
    copies = [
        pltpu.make_async_copy(source, target, sems.at[i])
        for i, (source, target) in enumerate(
            ((own_high_ref, own_high), (own_low_ref, own_low), (part_ref, total), (t_ref, tangent))
        )
    ]
    for copy in copies:
        copy.start()
    depth = stage.shape[0]

    for side, source in enumerate((low_ref, high_ref)):
        count = counts_ref[side]

        def fetch(i):
            slot = lax.rem(i, depth)
            return pltpu.make_async_copy(source.at[i], stage.at[slot], stage_sems.at[slot])

        for i in range(depth - 1):

            @pl.when(i < count)
            def _():
                fetch(i).start()

        def convert(i, carry):
            @pl.when(i + depth - 1 < count)
            def _():
                fetch(i + depth - 1).start()

            fetch(i).wait()
            high, low = halves(stage[lax.rem(i, depth)])
            far_high[side * room + i] = high
            far_low[side * room + i] = low
            return carry

        lax.fori_loop(0, count, convert, 0)

    for copy in copies:
        copy.wait()

    block = total.shape[1:]
    eye = lax.broadcasted_iota(I32, block, 0) == lax.broadcasted_iota(I32, block, 1)
    trace_ref[0, 0] = jnp.float32(0)

    def compute(q, carry):
        def term(m, carry):
            left = lists_ref[0, m]
            right = lists_ref[1, m]
            total[q] += product(own_high[left], own_low[left], far_high[right], far_low[right])
            return carry

        lax.fori_loop(lists_ref[2, q], lists_ref[2, q + 1], term, 0)

        @pl.when(q < stored)
        def _():
            at = jnp.minimum(q, stored - 1)
            scale = 1.5 * weight_ref[at].astype(F32)
            out_ref[at] = scale * tangent[at] - 0.5 * total[q]

        @pl.when((q >= stored) | (off_ref[jnp.minimum(q, stored - 1)] == 0))
        def _():
            trace_ref[0, 0] += jnp.sum(jnp.where(eye, total[q], 0.0))

        return carry

    lax.fori_loop(0, outs, compute, 0)


def halo_part(lists, counts, offsets, weights, low, high, own_high, own_low, part, t, rows, slots):
    smem = pl.BlockSpec(memory_space=pltpu.SMEM)
    vmem = pl.BlockSpec(memory_space=pltpu.VMEM)
    hbm = pl.BlockSpec(memory_space=pl.ANY)
    room = low.shape[0]
    stored = rows * slots
    block = t.shape[1:]
    return pl.pallas_call(
        functools.partial(halo_kernel, rows, slots, room),
        out_shape=(
            jax.ShapeDtypeStruct((stored,) + block, F32),
            jax.ShapeDtypeStruct((1, 1), F32),
        ),
        in_specs=[smem] * 4 + [hbm] * 6,
        out_specs=(vmem, smem),
        scratch_shapes=[
            pltpu.VMEM((4,) + block, F32),
            pltpu.VMEM((2 * room,) + block, BF16),
            pltpu.VMEM((2 * room,) + block, BF16),
            pltpu.VMEM((2 * stored,) + block, BF16),
            pltpu.VMEM((2 * stored,) + block, BF16),
            pltpu.VMEM((stored + rows,) + block, F32),
            pltpu.VMEM((stored,) + block, F32),
            pltpu.SemaphoreType.DMA((4,)),
            pltpu.SemaphoreType.DMA((4,)),
        ],
        compiler_params=pltpu.CompilerParams(vmem_limit_bytes=VMEM_LIMIT),
        cost_estimate=pl.CostEstimate(
            flops=60 * 3 * 2 * block[0] ** 3, bytes_accessed=30 * 2**20, transcendentals=0
        ),
        name="halo_rows",
    )(lists, counts, offsets, weights, low, high, own_high, own_low, part, t)


def body(density_blocks, density_live, tangent_blocks, tangent_live, block_offsets):
    rows, slots = density_live.shape
    block = density_blocks.shape[2:]
    n = lax.axis_size("row") * lax.axis_size("col")
    me = lax.axis_index(AXES).astype(I32)
    x = density_blocks.reshape((rows * slots,) + block)
    t = tangent_blocks.reshape((rows * slots,) + block)
    offsets = block_offsets.reshape(-1)
    weights = tangent_live.reshape(-1)

    meta = jnp.concatenate([density_live, tangent_live, block_offsets], axis=1)
    gathered = lax.all_gather(meta, AXES, tiled=True).reshape(n, rows, 3 * slots)
    plan = make_plan(gathered, me, slots)
    left, right = plan[:, 0], plan[:, 1]
    from_low, to_low = left[:CELLS], left[CELLS : 2 * CELLS]
    to_high, from_high = right[:CELLS], right[CELLS : 2 * CELLS]
    counts = jnp.stack([left[COUNT_ROW], right[COUNT_ROW + 1]])

    index = jnp.arange(rows * slots, dtype=I32).reshape(rows, slots, 1)
    here = block_offsets[:, :, None] == jnp.arange(-HALF, HALF + 1, dtype=I32)
    own = jnp.stack(
        [
            jnp.max(jnp.where(here & (live == 1)[:, :, None], index + shift, -1), axis=1)
            for live, shift in ((density_live, 0), (tangent_live, rows * slots))
        ]
    ).reshape(-1)

    forward = [(i, (i + 1) % n) for i in range(n)]
    backward = [(b, a) for a, b in forward]

    def with_room(room, own, left, right, offsets, weights, counts, to_high, to_low, x, t):
        forth, back = pack(own, to_high, to_low, x, t, room, rows)
        low = lax.ppermute(forth, AXES, forward)
        high = lax.ppermute(back, AXES, backward)
        part, own_high, own_low, lists = own_part(own, left, right, offsets, x, t, room, rows, slots)
        return halo_part(
            lists, counts, offsets, weights, low, high, own_high, own_low, part, t, rows, slots
        )

    worst = len(need_cells(0))
    rooms = [r for r in (12, 15, 16, 17, 18, 19, 20, 21, 22, 23, 24, 26) if r < worst] + [worst]
    choice = jnp.sum((left[COUNT_ROW + 2] > jnp.array(rooms[:-1], I32)).astype(I32))
    out, trace = lax.switch(
        choice,
        [functools.partial(with_room, room) for room in rooms],
        own, from_low, from_high, offsets, weights, counts, to_high, to_low, x, t,
    )
    mean_trace = lax.psum(trace[0, 0], AXES) / (rows * n)
    return out.reshape(tangent_blocks.shape), mean_trace


def solution(mesh):
    return jax.shard_map(
        body,
        mesh=mesh,
        in_specs=(
            P(AXES, None, None, None),
            P(AXES, None),
            P(AXES, None, None, None),
            P(AXES, None),
            P(AXES, None),
        ),
        out_specs=(P(AXES, None, None, None), P()),
        check_vma=False,
    )
```

```python
import functools

import jax
import jax.numpy as jnp
from jax import lax
from jax.experimental import pallas as pl
from jax.experimental.pallas import tpu as pltpu
from jax.sharding import PartitionSpec as P

HALF = 3
WIDTH = 2 * HALF + 1
WIN = 2 * HALF
AXES = ("row", "col")
VMEM_LIMIT = 58 * 1024 * 1024
F32 = jnp.float32
BF16 = jnp.bfloat16
I32 = jnp.int32


def need_cells(side):
    base = 0 if side == 0 else HALF
    return [
        (t, k, j)
        for t in range(2)
        for k in range(HALF)
        for j in range(WIN)
        if abs(j - (base + k)) <= HALF
    ]


def cell(t, k, j):
    return (t * HALF + k) * WIN + j


CELLS = 2 * HALF * WIN
RESULTS = HALF * WIN
CELL_ROW = (0, CELLS)
RESULT_ROW = (2 * CELLS, 2 * CELLS + RESULTS)
BIT_ROW = 2 * CELLS + 2 * RESULTS
COUNT_ROW = (BIT_ROW + WIN, BIT_ROW + WIN + 1)
CROSS_ROW = (BIT_ROW + WIN + 2, BIT_ROW + WIN + 3)
SUM_ROW = (BIT_ROW + WIN + 4, BIT_ROW + WIN + 5)
TOP_ROW = BIT_ROW + WIN + 6
PLAN_ROWS = 128


def split_room(room):
    first, last = (room + 1) // 2, room * 3 // 8
    return first, room - first - last, last


def room_for_sums(sums):
    return ((8 * sums + 2) * 171) >> 9


def either(flags):
    return functools.reduce(jnp.bitwise_or, flags)


def plan_kernel(slots, me_ref, meta_ref, out_ref, table):
    n = meta_ref.shape[-1]
    fields = 3 * slots

    def row(i, f):
        source, r = (0, i) if i < HALF else (1, i - HALF)
        at = r * fields + f
        return meta_ref[source, at : at + 1, :]

    one = jnp.ones((1, n), I32)
    zero = jnp.zeros((1, n), I32)
    live = [{}, {}]
    kept, shown = {}, {}
    for i in range(WIN):
        offs = [row(i, 2 * slots + s) for s in range(slots)]
        flags = [[jnp.where(row(i, t * slots + s) == 1, one, zero) for s in range(slots)] for t in range(2)]
        for j in range(WIN):
            d = j - i
            if abs(d) > HALF:
                continue
            here = [jnp.where(o == d, one, zero) for o in offs]
            kept[i, j] = either(here)
            shown[i, j] = one if d == 0 else kept[i, j]
            for t in range(2):
                live[t][i, j] = either([h & f for h, f in zip(here, flags[t])])

    def near(*pairs):
        return all(abs(p - q) <= HALF for p, q in pairs)

    as_left = {}
    for side in range(2):
        base, other = (0, HALF) if side == 0 else (HALF, 0)
        for t, k, j in need_cells(side):
            if other <= j < other + HALF:
                ends = [
                    live[1 - t][j, e] & shown[base + k, e] for e in range(WIN) if near((e, j), (e, base + k))
                ]
                as_left[side, t, k, j] = live[t][base + k, j] & either(ends)
    sums = {}
    for side in range(2):
        base, other = (0, HALF) if side == 0 else (HALF, 0)
        for i in range(other, other + HALF):
            for j in range(WIN):
                if near((i, j)):
                    terms = [
                        live[t][i, k] & live[1 - t][k, j]
                        for t in range(2)
                        for k in range(base, base + HALF)
                        if near((i, k), (k, j))
                    ]
                    if terms:
                        sums[side, i, j] = kept[i, j] & either(terms)

    def visit(bits, on_cell, on_sum):
        for side in range(2):
            base, other = (0, HALF) if side == 0 else (HALF, 0)

            def is_cross(spec):
                return other <= spec[2] < other + HALF

            for spec in sorted(need_cells(side), key=lambda c: not is_cross(c)):
                t, k, j = spec
                kk = base + k
                users = [
                    live[1 - t][i, kk] & shown[i, j] & (1 - bits[i])
                    for i in range(other, other + HALF)
                    if near((i, kk), (i, j))
                ]
                need = either(users) & live[t][kk, j]
                if is_cross(spec):
                    need = need | (bits[kk] & as_left[side, t, k, j])
                on_cell(side, spec, is_cross(spec), need)
            for i in range(other, other + HALF):
                for j in range(WIN):
                    if (side, i, j) in sums:
                        on_sum(side, i - other, j, sums[side, i, j] & bits[i])

    trials = 2**WIN
    trial = lax.broadcasted_iota(I32, (trials, n), 0)
    totals = {}

    def tally(name, side, value):
        totals[name, side] = totals[name, side] + value if (name, side) in totals else value

    def count_cell(side, spec, cross, need):
        tally("all", side, need)
        if cross:
            tally("cross", side, need)

    visit(
        [(trial >> i) & 1 for i in range(WIN)],
        count_cell,
        lambda side, i, j, need: tally("sum", side, need),
    )
    cost = jnp.zeros((trials, n), I32)
    load = jnp.zeros((trials, n), I32)
    for side in range(2):
        both = totals["all", side] + totals["sum", side]
        load = load + both
        cost = jnp.maximum(cost, both)
        cost = jnp.maximum(cost, 2 * totals["cross", side] - 1)
        cost = jnp.maximum(cost, room_for_sums(totals["sum", side]))
    score = ((cost * 256 + load) * trials + trial).astype(F32)
    best = jnp.min(score, axis=0, keepdims=True)
    best = best.astype(I32)
    bits = [(best >> i) & 1 for i in range(WIN)]
    top = jnp.max((best >> (8 + WIN)).astype(F32), axis=1, keepdims=True).astype(I32)

    table[...] = jnp.full(table.shape, -1, I32)

    def put(at, value):
        table[at : at + 1, :] = value

    counts = {key: zero for key in [(name, side) for name in ("all", "cross", "sum") for side in range(2)]}

    def place_cell(side, spec, cross, need):
        put(CELL_ROW[side] + cell(*spec), jnp.where(need == 1, counts["all", side], -one))
        counts["all", side] = counts["all", side] + need
        if cross:
            counts["cross", side] = counts["cross", side] + need

    def place_sum(side, i, j, need):
        put(RESULT_ROW[side] + i * WIN + j, jnp.where(need == 1, counts["sum", side], -one))
        counts["sum", side] = counts["sum", side] + need

    visit(bits, place_cell, place_sum)
    for i in range(WIN):
        put(BIT_ROW + i, bits[i])
    for side in range(2):
        put(COUNT_ROW[side], counts["all", side])
        put(CROSS_ROW[side], counts["cross", side])
        put(SUM_ROW[side], counts["sum", side])
    put(TOP_ROW, jnp.broadcast_to(top, (1, n)))

    me = me_ref[0]
    whole = table[...]
    lane = lax.broadcasted_iota(I32, whole.shape, 1)
    right = lax.rem(me + 1, n)
    first = jnp.sum(jnp.where(lane == me, whole, 0), axis=1, keepdims=True)
    second = jnp.sum(jnp.where(lane == right, whole, 0), axis=1, keepdims=True)
    out_lane = lax.broadcasted_iota(I32, out_ref.shape, 1)
    out_ref[...] = jnp.where(out_lane == 0, first, second)


def make_plan(meta, me, slots):
    n, rows = meta.shape[0], meta.shape[1]
    low = jnp.roll(meta[:, rows - HALF :], 1, axis=0).reshape(n, -1).T
    high = meta[:, :HALF].reshape(n, -1).T
    return pl.pallas_call(
        functools.partial(plan_kernel, slots),
        out_shape=jax.ShapeDtypeStruct((PLAN_ROWS, 128), I32),
        in_specs=[pl.BlockSpec(memory_space=pltpu.SMEM), pl.BlockSpec(memory_space=pltpu.VMEM)],
        out_specs=pl.BlockSpec(memory_space=pltpu.VMEM),
        scratch_shapes=[pltpu.VMEM((PLAN_ROWS, n), I32)],
        name="plan",
    )(me.reshape(1), jnp.stack([low, high]))


SMEM = pl.BlockSpec(memory_space=pltpu.SMEM)
VMEM = pl.BlockSpec(memory_space=pltpu.VMEM)
HBM = pl.BlockSpec(memory_space=pl.ANY)
SENT = 2 * HALF * WIN + 1


def over(count, act, begin=0):
    def step(i, carry):
        act(i)
        return carry

    lax.fori_loop(begin, count, step, 0)


def list_sent(rows, own_ref, left_ref, right_ref, sent_ref):
    for side, plan_ref in ((0, right_ref), (1, left_ref)):
        for t, k, j in need_cells(side):
            own_row = rows - HALF + k if side == 0 else k
            place = j - k + HALF if side == 0 else j - k
            at = plan_ref[CELL_ROW[side] + cell(t, k, j)]
            at = jnp.where(at >= 0, at, SENT - 1)
            sent_ref[side * SENT + at] = own_ref[(t * rows + own_row) * WIDTH + place]


class Carrier:
    def __init__(self, side, low, high, shift, sent_ref, x_ref, t_ref, out, held, sems_in, sems_out):
        self.side, self.low, self.count, self.shift = side, low, jnp.maximum(high - low, 0), shift
        self.sent_ref, self.sources, self.out, self.held = sent_ref, (x_ref, t_ref), out, held
        self.sems_in, self.sems_out = sems_in, sems_out

    def arrival(self, t, block, i):
        return pltpu.make_async_copy(self.sources[t].at[block], self.held.at[self.side, i], self.sems_in.at[self.side, i])

    def departure(self, i):
        target = self.out.at[self.shift + i]
        return pltpu.make_async_copy(self.held.at[self.side, i], target, self.sems_out.at[self.side, i])

    def begin(self):
        stored = self.sources[0].shape[0]

        def act(i):
            block = self.sent_ref[self.side * SENT + self.low + i]
            for t in range(2):

                @pl.when((block >= stored) == (t == 1))
                def _():
                    self.arrival(t, block - t * stored, i).start()

        over(self.count, act)

    def onward(self):
        def act(i):
            self.arrival(0, 0, i).wait()
            self.departure(i).start()

        over(self.count, act)

    def end(self):
        over(self.count, lambda i: self.departure(i).wait())


def pack_kernel(rows, low, high, own_ref, left_ref, right_ref, x_ref, t_ref, forth_out, back_out, sent_ref, held, sems_in, sems_out):
    list_sent(rows, own_ref, left_ref, right_ref, sent_ref)
    carriers = [
        Carrier(side, low, jnp.minimum(count, high), 0, sent_ref, x_ref, t_ref, out, held, sems_in, sems_out)
        for side, count, out in (
            (0, right_ref[COUNT_ROW[0]], forth_out),
            (1, left_ref[COUNT_ROW[1]], back_out),
        )
    ]
    for carrier in carriers:
        carrier.begin()
    for carrier in carriers:
        carrier.onward()
    for carrier in carriers:
        carrier.end()


def pack(own, left, right, x, t, low, high, rows):
    block = x.shape[1:]
    room = high - low
    shape = jax.ShapeDtypeStruct((room,) + block, F32)
    return pl.pallas_call(
        functools.partial(pack_kernel, rows, low, high),
        out_shape=(shape, shape, jax.ShapeDtypeStruct((2 * SENT,), I32)),
        in_specs=[SMEM] * 3 + [HBM] * 2,
        out_specs=(HBM, HBM, SMEM),
        scratch_shapes=[
            pltpu.VMEM((2, room) + block, F32),
            pltpu.SemaphoreType.DMA((2, room)),
            pltpu.SemaphoreType.DMA((2, room)),
        ],
        compiler_params=pltpu.CompilerParams(vmem_limit_bytes=VMEM_LIMIT),
        name="pack",
    )(own, left, right, x, t)


def halves(values):
    high = values.astype(BF16)
    return high, (values - high.astype(F32)).astype(BF16)


STRIPE = 32


def stripes(block, act):
    over(block[0] // STRIPE, lambda i: act(pl.ds(pl.multiple_of(i * STRIPE, STRIPE), STRIPE)))


def split_block(source, at, high_ref, low_ref, to):
    def act(part):
        high_ref[to, part, :], low_ref[to, part, :] = halves(source[at, part, :])

    stripes(source.shape[1:], act)


def add_product(total, at, sign, lh, ll, i, rh, rl, j):
    dot = functools.partial(jnp.dot, preferred_element_type=F32)
    half = total.shape[-2] // 2

    def act(h):
        part = pl.ds(pl.multiple_of(h * half, half), half)
        high, low = lh[i, part, :], ll[i, part, :]
        result = dot(high, rh[j]) + (dot(high, rl[j]) + dot(low, rh[j]))
        total[at, part, :] += result if sign == 1 else sign * result

    over(2, act)


OWN, FIRST, LAST, HELP = range(4)
LEFT, RIGHT, BEGIN = range(3)


def list_length(rows, slots):
    return -(-((rows * slots + rows) * 2 * WIDTH + 1) // 128) * 128


def own_kernel(
    rows, slots, room_a, room_c, room_b,
    own_ref, left_ref, right_ref, off_ref, x_ref, t_ref,
    part_ref, high_ref, low_ref, lists_ref, used_ref,
):
    stored = rows * slots
    outs = stored + rows
    early = room_a + room_c
    late = [left_ref[SUM_ROW[0]] - early, room_b + right_ref[SUM_ROW[1]] - early]

    def clear(i, carry):
        used_ref[i] = 0
        return carry

    lax.fori_loop(0, 2 * stored, clear, 0)

    def of_output(q, counts):
        is_diag = q >= stored
        row = jnp.where(is_diag, q - stored, lax.div(q, slots))
        d = jnp.where(is_diag, 0, off_ref[jnp.minimum(q, stored - 1)])
        has_zero = jnp.bool_(False)
        for s in range(slots):
            has_zero = has_zero | (off_ref[row * slots + s] == 0)
        wanted = jnp.logical_not(is_diag & has_zero)
        for which in (OWN, FIRST, LAST):
            lists_ref[which, BEGIN, q] = counts[which]
        low_row = row - (rows - HALF)
        left_open = (row < HALF) & (left_ref[BIT_ROW + HALF + jnp.minimum(row, HALF - 1)] == 0)
        right_open = (low_row >= 0) & (right_ref[BIT_ROW + jnp.maximum(low_row, 0)] == 0)
        column = row + d

        def of_term(m, counts):
            t = lax.rem(m, 2)
            e = lax.div(m, 2) - HALF
            k = row + e
            place = d - e + HALF
            ok = wanted & (place >= 0) & (place < WIDTH)
            left = own_ref[(t * rows + row) * WIDTH + e + HALF]
            ok = ok & (left >= 0)
            is_own = ok & (k >= 0) & (k < rows)
            is_low = ok & (k < 0) & left_open
            is_high = ok & (k >= rows) & right_open
            own_block = own_ref[jnp.where(is_own, ((1 - t) * rows + k) * WIDTH + place, 0)]
            low_at = ((1 - t) * HALF + k + HALF) * WIN + column + HALF
            low_block = left_ref[CELL_ROW[0] + jnp.where(is_low, low_at, 0)]
            high_at = ((1 - t) * HALF + k - rows) * WIN + column - rows + HALF
            high_block = right_ref[CELL_ROW[1] + jnp.where(is_high, high_at, 0)]
            far_block = jnp.where(is_low, low_block, high_block)
            far_ok = (is_low | is_high) & (far_block >= 0)
            own_count, first_count, last_count = counts
            lists_ref[OWN, LEFT, own_count] = left
            lists_ref[OWN, RIGHT, own_count] = own_block
            own_count = own_count + jnp.where(is_own & (own_block >= 0), 1, 0)
            lists_ref[FIRST, LEFT, first_count] = left
            lists_ref[FIRST, RIGHT, first_count] = far_block + jnp.where(is_low, 0, early)
            first_count = first_count + jnp.where(far_ok & (far_block < early), 1, 0)
            lists_ref[LAST, LEFT, last_count] = left
            lists_ref[LAST, RIGHT, last_count] = far_block + jnp.where(is_low, late[0], late[1])
            is_last = far_ok & (far_block >= early)
            last_count = last_count + jnp.where(is_last, 1, 0)

            @pl.when(is_last)
            def _():
                used_ref[left] = 1

            return own_count, first_count, last_count

        return lax.fori_loop(0, 2 * WIDTH, of_term, counts)

    ends = lax.fori_loop(0, outs, of_output, (jnp.int32(0),) * 3)
    for which in (OWN, FIRST, LAST):
        lists_ref[which, BEGIN, outs] = ends[which]

    count = jnp.int32(0)
    for side, plan_ref in ((0, right_ref), (1, left_ref)):
        base, other = (0, HALF) if side == 0 else (HALF, 0)
        shift = rows - HALF if side == 0 else 0

        def of_sum(q, count):
            i = lax.div(q, WIN)
            j = lax.rem(q, WIN)
            open_row = plan_ref[BIT_ROW + other + i] == 1
            shown = (plan_ref[RESULT_ROW[side] + q] >= 0) | (j == other + i)
            open_row = open_row & shown
            lists_ref[HELP, BEGIN, side * RESULTS + q] = count

            def of_term(m, count):
                t = lax.rem(m, 2)
                k = lax.div(m, 2)
                reach = j - (base + k)
                ok = open_row & (reach >= -HALF) & (reach <= HALF)
                across = other + i - (base + k)
                ok = ok & (across >= -HALF) & (across <= HALF)
                left = plan_ref[CELL_ROW[1 - side] + (t * HALF + i) * WIN + base + k]
                right_at = jnp.where(ok, ((1 - t) * rows + shift + k) * WIDTH + reach + HALF, 0)
                right = own_ref[right_at]
                lists_ref[HELP, LEFT, count] = left + (room_a if side == 0 else 0)
                lists_ref[HELP, RIGHT, count] = right
                return count + jnp.where(ok & (left >= 0) & (right >= 0), 1, 0)

            return lax.fori_loop(0, 2 * HALF, of_term, count)

        count = lax.fori_loop(0, RESULTS, of_sum, count)
    lists_ref[HELP, BEGIN, 2 * RESULTS] = count

    def split(i, carry):
        for t, source in enumerate((x_ref, t_ref)):
            split_block(source, i, high_ref, low_ref, t * stored + i)
        return carry

    lax.fori_loop(0, stored, split, 0)

    def compute(q, carry):
        part_ref[q] = jnp.zeros(part_ref.shape[1:], F32)

        def term(m, carry):
            left = lists_ref[OWN, LEFT, m]
            right = lists_ref[OWN, RIGHT, m]
            add_product(part_ref, q, 1, high_ref, low_ref, left, high_ref, low_ref, right)
            return carry

        return lax.fori_loop(lists_ref[OWN, BEGIN, q], lists_ref[OWN, BEGIN, q + 1], term, carry)

    lax.fori_loop(0, outs, compute, 0)


def own_part(own, left, right, offsets, x, t, room_a, room_c, room_b, rows, slots):
    stored = rows * slots
    block = x.shape[1:]
    length = list_length(rows, slots)
    return pl.pallas_call(
        functools.partial(own_kernel, rows, slots, room_a, room_c, room_b),
        out_shape=(
            jax.ShapeDtypeStruct((stored + rows,) + block, F32),
            jax.ShapeDtypeStruct((2 * stored,) + block, BF16),
            jax.ShapeDtypeStruct((2 * stored,) + block, BF16),
            jax.ShapeDtypeStruct((4, 3, length), I32),
            jax.ShapeDtypeStruct((2 * stored,), I32),
        ),
        in_specs=[SMEM] * 4 + [VMEM] * 2,
        out_specs=(VMEM, VMEM, VMEM, SMEM, SMEM),
        compiler_params=pltpu.CompilerParams(vmem_limit_bytes=VMEM_LIMIT),
        cost_estimate=pl.CostEstimate(
            flops=2**20, bytes_accessed=2**16, transcendentals=0
        ),
        name="own_rows",
    )(own, left, right, offsets, x, t)


def convert_blocks(source, count, shift, far_high, far_low, stage, stage_sems):
    depth = stage.shape[0]

    def fetch(i):
        slot = lax.rem(i, depth)
        return pltpu.make_async_copy(source.at[i], stage.at[slot], stage_sems.at[slot])

    for i in range(depth - 1):

        @pl.when(i < count)
        def _():
            fetch(i).start()

    def convert(i, carry):
        @pl.when(i + depth - 1 < count)
        def _():
            fetch(i + depth - 1).start()

        fetch(i).wait()
        split_block(stage, lax.rem(i, depth), far_high, far_low, shift + i)
        return carry

    lax.fori_loop(0, count, convert, 0)


def trace_of(ref, at):
    side = ref.shape[-1]

    def stripe(i, total):
        first = pl.multiple_of(i * STRIPE, STRIPE)
        row = lax.broadcasted_iota(I32, (STRIPE, side), 0) + first
        column = lax.broadcasted_iota(I32, (STRIPE, side), 1)
        return total + jnp.where(row == column, ref[at, pl.ds(first, STRIPE), :], 0.0)

    return jnp.sum(lax.fori_loop(0, side // STRIPE, stripe, jnp.zeros((STRIPE, side), F32)))


def help_kernel(
    rows, room_a, early, room_b,
    sent_ref, left_ref, right_ref, lists_ref,
    low_ref, high_ref, own_high_ref, own_low_ref, x_ref, t_ref,
    forth_out, back_out, trace_ref,
    stage, far_high, far_low, own_high, own_low, sums, held, stage_sems, sems, sum_sems, sems_in, sems_out,
):
    outs = (forth_out, back_out)
    copies = [
        pltpu.make_async_copy(source, target, sems.at[i])
        for i, (source, target) in enumerate(((own_high_ref, own_high), (own_low_ref, own_low)))
    ]
    helps = lists_ref[HELP, BEGIN, 2 * RESULTS] > 0

    @pl.when(helps)
    def _():
        for copy in copies:
            copy.start()

    shifts = (right_ref[SUM_ROW[0]], left_ref[SUM_ROW[1]])
    carriers = [
        Carrier(side, early, count, shifts[side], sent_ref, x_ref, t_ref, outs[side], held, sems_in, sems_out)
        for side, count in ((0, right_ref[COUNT_ROW[0]]), (1, left_ref[COUNT_ROW[1]]))
    ]
    for carrier in carriers:
        carrier.begin()
    trace_ref[0, 0] = jnp.float32(0)

    @pl.when(helps)
    def _():
        convert_blocks(low_ref, left_ref[CROSS_ROW[0]], 0, far_high, far_low, stage, stage_sems)
        convert_blocks(high_ref, right_ref[CROSS_ROW[1]], room_a, far_high, far_low, stage, stage_sems)
        for copy in copies:
            copy.wait()

    for carrier in carriers:
        carrier.onward()
    for side, plan_ref in ((0, right_ref), (1, left_ref)):
        other = HALF if side == 0 else 0

        def compute(q, carry):
            begin_at = lists_ref[HELP, BEGIN, side * RESULTS + q]
            end_at = lists_ref[HELP, BEGIN, side * RESULTS + q + 1]
            at = plan_ref[RESULT_ROW[side] + q]

            @pl.when(end_at > begin_at)
            def _():
                slot = jnp.where(at >= 0, at, room_b)
                sums[side, slot] = jnp.zeros(sums.shape[2:], F32)

                def term(m, carry):
                    left = lists_ref[HELP, LEFT, m]
                    right = lists_ref[HELP, RIGHT, m]
                    add_product(sums.at[side], slot, 1, far_high, far_low, left, own_high, own_low, right)
                    return carry

                lax.fori_loop(begin_at, end_at, term, 0)

                @pl.when(at >= 0)
                def _():
                    pltpu.make_async_copy(sums.at[side, slot], outs[side].at[slot], sum_sems.at[side, slot]).start()

                @pl.when(lax.rem(q, WIN) == other + lax.div(q, WIN))
                def _():
                    trace_ref[0, 0] += trace_of(sums.at[side], slot)

            return carry

        lax.fori_loop(0, RESULTS, compute, 0)
    for side in range(2):

        def finish(i, carry):
            pltpu.make_async_copy(sums.at[side, i], outs[side].at[i], sum_sems.at[side, i]).wait()
            return carry

        lax.fori_loop(0, shifts[side], finish, 0)
    for carrier in carriers:
        carrier.end()


def help_part(sent, left, right, lists, low, high, own_high, own_low, x, t, early, room_b, rows):
    room_a = low.shape[0]
    block = x.shape[1:]
    stored = x.shape[0]
    shape = jax.ShapeDtypeStruct((room_b,) + block, F32)
    return pl.pallas_call(
        functools.partial(help_kernel, rows, room_a, early, room_b),
        out_shape=(shape, shape, jax.ShapeDtypeStruct((1, 1), F32)),
        in_specs=[SMEM] * 4 + [HBM] * 6,
        out_specs=(HBM, HBM, SMEM),
        scratch_shapes=[
            pltpu.VMEM((4,) + block, F32),
            pltpu.VMEM((2 * room_a,) + block, BF16),
            pltpu.VMEM((2 * room_a,) + block, BF16),
            pltpu.VMEM((2 * stored,) + block, BF16),
            pltpu.VMEM((2 * stored,) + block, BF16),
            pltpu.VMEM((2, room_b + 1) + block, F32),
            pltpu.VMEM((2, room_b) + block, F32),
            pltpu.SemaphoreType.DMA((4,)),
            pltpu.SemaphoreType.DMA((2,)),
            pltpu.SemaphoreType.DMA((2, room_b)),
            pltpu.SemaphoreType.DMA((2, room_b)),
            pltpu.SemaphoreType.DMA((2, room_b)),
        ],
        compiler_params=pltpu.CompilerParams(vmem_limit_bytes=VMEM_LIMIT),
        cost_estimate=pl.CostEstimate(
            flops=2**20, bytes_accessed=2**16, transcendentals=0
        ),
        name="help_rows",
)(sent, left, right, lists, low, high, own_high, own_low, x, t)


def first_kernel(
    rows, slots, room_a, room_c,
    lists_ref, left_ref, right_ref, off_ref, weight_ref,
    low_ref, high_ref, low_ref_2, high_ref_2, own_high_ref, own_low_ref, part_ref, t_ref,
    out_ref, trace_ref,
    stage, far_high, far_low, own_high, own_low, total, tangent, stage_sems, sems,
):
    stored = rows * slots
    outs = stored + rows
    copies = [
        pltpu.make_async_copy(source, target, sems.at[i])
        for i, (source, target) in enumerate(
            ((own_high_ref, own_high), (own_low_ref, own_low), (part_ref, total), (t_ref, tangent))
        )
    ]
    for copy in copies:
        copy.start()
    early = room_a + room_c
    for side, (source, source_2, plan_ref) in enumerate(
        ((low_ref, low_ref_2, left_ref), (high_ref, high_ref_2, right_ref))
    ):
        whole = plan_ref[COUNT_ROW[side]]
        convert_blocks(source, jnp.minimum(whole, room_a), side * early, far_high, far_low, stage, stage_sems)
        count = jnp.maximum(jnp.minimum(whole, early) - room_a, 0)
        convert_blocks(source_2, count, side * early + room_a, far_high, far_low, stage, stage_sems)
    for copy in copies:
        copy.wait()

    trace_ref[0, 0] = jnp.float32(0)

    def compute(q, carry):
        def term(m, carry):
            left = lists_ref[FIRST, LEFT, m]
            right = lists_ref[FIRST, RIGHT, m]
            add_product(total, q, 1, own_high, own_low, left, far_high, far_low, right)
            return carry

        lax.fori_loop(lists_ref[FIRST, BEGIN, q], lists_ref[FIRST, BEGIN, q + 1], term, 0)

        @pl.when(q < stored)
        def _():
            at = jnp.minimum(q, stored - 1)
            scale = 1.5 * weight_ref[at].astype(F32)

            def act(part):
                out_ref[at, part, :] = scale * tangent[at, part, :] - 0.5 * total[q, part, :]

            stripes(total.shape[1:], act)

        @pl.when((q >= stored) | (off_ref[jnp.minimum(q, stored - 1)] == 0))
        def _():
            trace_ref[0, 0] += trace_of(total, q)

        return carry

    lax.fori_loop(0, outs, compute, 0)


def first_part(lists, left, right, offsets, weights, low, high, low_2, high_2, own_high, own_low, part, t, rows, slots):
    room_a, room_c = low.shape[0], low_2.shape[0]
    room = room_a + room_c
    stored = rows * slots
    block = t.shape[1:]
    return pl.pallas_call(
        functools.partial(first_kernel, rows, slots, room_a, room_c),
        out_shape=(
            jax.ShapeDtypeStruct((stored,) + block, F32),
            jax.ShapeDtypeStruct((1, 1), F32),
        ),
        in_specs=[SMEM] * 5 + [HBM] * 8,
        out_specs=(VMEM, SMEM),
        scratch_shapes=[
            pltpu.VMEM((4,) + block, F32),
            pltpu.VMEM((2 * room,) + block, BF16),
            pltpu.VMEM((2 * room,) + block, BF16),
            pltpu.VMEM((2 * stored,) + block, BF16),
            pltpu.VMEM((2 * stored,) + block, BF16),
            pltpu.VMEM((stored + rows,) + block, F32),
            pltpu.VMEM((stored,) + block, F32),
            pltpu.SemaphoreType.DMA((4,)),
            pltpu.SemaphoreType.DMA((4,)),
        ],
        compiler_params=pltpu.CompilerParams(vmem_limit_bytes=VMEM_LIMIT),
        cost_estimate=pl.CostEstimate(
            flops=2**20, bytes_accessed=2**16, transcendentals=0
        ),
        name="first_halo",
    )(lists, left, right, offsets, weights, low, high, low_2, high_2, own_high, own_low, part, t)


def last_kernel(
    rows, slots, early, room_b,
    lists_ref, used_ref, left_ref, right_ref, off_ref,
    low_ref, high_ref, own_high_ref, own_low_ref, given_ref,
    out_ref,
    got, far_high, far_low, own_high, own_low, held, got_sems, own_sems, in_sems, out_sems,
):
    stored = rows * slots
    plans = (left_ref, right_ref)
    sources = (low_ref, high_ref)
    sum_counts = [plans[side][SUM_ROW[side]] for side in range(2)]
    counts = [
        sum_counts[side] + jnp.maximum(plans[side][COUNT_ROW[side]] - early, 0) for side in range(2)
    ]

    def fetch(side, i):
        return pltpu.make_async_copy(sources[side].at[i], got.at[side, i], got_sems.at[side, i])

    def places(q):
        row = lax.div(q, slots)
        column = row + off_ref[q]
        low_ok = (row < HALF) & (column < HALF)
        low_at = left_ref[RESULT_ROW[0] + jnp.where(low_ok, row * WIN + column + HALF, 0)]
        low_at = jnp.where(low_ok, low_at, -1)
        base = rows - HALF
        high_ok = (row >= base) & (column >= base)
        high_at = right_ref[RESULT_ROW[1] + jnp.where(high_ok, (row - base) * WIN + column - base, 0)]
        high_at = jnp.where(high_ok, high_at, -1)
        begin, end = lists_ref[LAST, BEGIN, q], lists_ref[LAST, BEGIN, q + 1]
        return low_at, high_at, begin, end

    def touched(q):
        low_at, high_at, begin, end = places(q)
        return (low_at >= 0) | (high_at >= 0) | (end > begin)

    def load(q):
        return pltpu.make_async_copy(given_ref.at[q], held.at[q], in_sems.at[q])

    def store(q):
        return pltpu.make_async_copy(held.at[q], out_ref.at[q], out_sems.at[q])

    for side in range(2):
        over(counts[side], lambda i, side=side: fetch(side, i).start())

    def when_touched(act):
        def step(q):
            @pl.when(touched(q))
            def _():
                act(q)

        return step

    over(stored, when_touched(lambda q: load(q).start()))

    def own_copies(i):
        return (
            pltpu.make_async_copy(own_high_ref.at[i], own_high.at[i], own_sems.at[0, i]),
            pltpu.make_async_copy(own_low_ref.at[i], own_low.at[i], own_sems.at[1, i]),
        )

    def on_used(act):
        def step(i):
            @pl.when(used_ref[i] == 1)
            def _():
                for copy in own_copies(i):
                    act(copy)

        over(2 * stored, step)

    on_used(lambda copy: copy.start())
    for side in range(2):
        over(counts[side], lambda i, side=side: fetch(side, i).wait())

        def convert(i, carry):
            split_block(got.at[side], i, far_high, far_low, side * room_b + i)
            return carry

        lax.fori_loop(sum_counts[side], counts[side], convert, 0)
    on_used(lambda copy: copy.wait())

    def compute(q):
        low_at, high_at, begin, end = places(q)
        load(q).wait()

        @pl.when(low_at >= 0)
        def _():
            held[q] -= 0.5 * got[0, low_at]

        @pl.when(high_at >= 0)
        def _():
            held[q] -= 0.5 * got[1, high_at]

        def term(m, carry):
            left = lists_ref[LAST, LEFT, m]
            right = lists_ref[LAST, RIGHT, m]
            add_product(held, q, -0.5, own_high, own_low, left, far_high, far_low, right)
            return carry

        lax.fori_loop(begin, end, term, 0)
        store(q).start()

    over(stored, when_touched(compute))
    over(stored, when_touched(lambda q: store(q).wait()))


def last_part(lists, used, left, right, offsets, low, high, own_high, own_low, given, early, rows, slots):
    room_b = low.shape[0]
    stored = rows * slots
    block = given.shape[1:]
    return pl.pallas_call(
        functools.partial(last_kernel, rows, slots, early, room_b),
        out_shape=jax.ShapeDtypeStruct(given.shape, F32),
        in_specs=[SMEM] * 5 + [HBM] * 5,
        out_specs=HBM,
        input_output_aliases={9: 0},
        scratch_shapes=[
            pltpu.VMEM((2, room_b) + block, F32),
            pltpu.VMEM((2 * room_b,) + block, BF16),
            pltpu.VMEM((2 * room_b,) + block, BF16),
            pltpu.VMEM((2 * stored,) + block, BF16),
            pltpu.VMEM((2 * stored,) + block, BF16),
            pltpu.VMEM((stored,) + block, F32),
            pltpu.SemaphoreType.DMA((2, room_b)),
            pltpu.SemaphoreType.DMA((2, 2 * stored)),
            pltpu.SemaphoreType.DMA((stored,)),
            pltpu.SemaphoreType.DMA((stored,)),
        ],
        compiler_params=pltpu.CompilerParams(vmem_limit_bytes=VMEM_LIMIT),
        cost_estimate=pl.CostEstimate(
            flops=2**20, bytes_accessed=2**16, transcendentals=0
        ),
        name="last_halo",
    )(lists, used, left, right, offsets, low, high, own_high, own_low, given)


def partners(value, n, step):
    return lax.ppermute(value, AXES, [(i, i ^ step) for i in range(n)])


def steps_of(n):
    step = 1
    while step < n:
        yield (step, 2 * step, 3 * step) if 2 * step < n else (step,)
        step *= 4


def gather_all(value, n):
    if n & (n - 1):
        return lax.all_gather(value, AXES)
    value = value[None]
    for steps in steps_of(n):
        value = jnp.concatenate([value] + [partners(value, n, step) for step in steps])
    me = lax.axis_index(AXES)
    step = 1
    while step < n:
        pairs = value.reshape((n // (2 * step), 2, step) + value.shape[1:])
        value = jnp.where((me // step) % 2 == 0, pairs, pairs[:, ::-1]).reshape(value.shape)
        step *= 2
    return value


def sum_all(value, n):
    if n & (n - 1):
        return lax.psum(value, AXES)
    for steps in steps_of(n):
        others = [partners(value, n, step) for step in steps]
        value = value + others[0]
        if len(others) > 1:
            value = value + (others[1] + others[2])
    return value


def body(density_blocks, density_live, tangent_blocks, tangent_live, block_offsets):
    rows, slots = density_live.shape
    block = density_blocks.shape[2:]
    n = lax.axis_size("row") * lax.axis_size("col")
    me = lax.axis_index(AXES).astype(I32)
    x = density_blocks.reshape((rows * slots,) + block)
    t = tangent_blocks.reshape((rows * slots,) + block)
    offsets = block_offsets.reshape(-1)
    weights = tangent_live.reshape(-1)

    meta = jnp.concatenate([density_live, tangent_live, block_offsets], axis=1)
    gathered = gather_all(meta, n)
    plan = make_plan(gathered, me, slots)
    left, right = plan[:, 0], plan[:, 1]

    index = jnp.arange(rows * slots, dtype=I32).reshape(rows, slots, 1)
    here = block_offsets[:, :, None] == jnp.arange(-HALF, HALF + 1, dtype=I32)
    own = jnp.stack(
        [
            jnp.max(jnp.where(here & (live == 1)[:, :, None], index + shift, -1), axis=1)
            for live, shift in ((density_live, 0), (tangent_live, rows * slots))
        ]
    ).reshape(-1)

    forward = [(i, (i + 1) % n) for i in range(n)]
    backward = [(b, a) for a, b in forward]

    def exchange(forth, back):
        return lax.ppermute(forth, AXES, forward), lax.ppermute(back, AXES, backward)

    def with_room(room, own, left, right, offsets, weights, x, t):
        room_a, room_c, room_b = split_room(room)
        early = room_a + room_c
        forth, back, sent = pack(own, left, right, x, t, 0, room_a, rows)
        low, high = exchange(forth, back)
        forth, back, _ = pack(own, left, right, x, t, room_a, early, rows)
        low_2, high_2 = exchange(forth, back)
        own, _, _ = lax.optimization_barrier((own, forth, back))
        part, own_high, own_low, lists, used = own_part(
            own, left, right, offsets, x, t, room_a, room_c, room_b, rows, slots
        )
        forth, back, help_trace = help_part(
            sent, left, right, lists, low, high, own_high, own_low, x, t, early, room_b, rows
        )
        forth, back, low_2, high_2 = lax.optimization_barrier((forth, back, low_2, high_2))
        last_low, last_high = exchange(forth, back)
        given, trace = first_part(
            lists, left, right, offsets, weights, low, high, low_2, high_2, own_high, own_low, part, t, rows, slots
        )
        trace = sum_all(trace + help_trace, n)
        out = last_part(
            lists, used, left, right, offsets, last_low, last_high, own_high, own_low, given, early, rows, slots
        )
        return out, trace

    worst = len(need_cells(0))
    rooms = [r for r in (12, 13, 14, 15, 16, 17, 18, 19, 20, 22, 25) if r < worst] + [worst]
    choice = jnp.sum((left[TOP_ROW] > jnp.array(rooms[:-1], I32)).astype(I32))
    out, trace = lax.switch(
        choice,
        [functools.partial(with_room, room) for room in rooms],
        own, left, right, offsets, weights, x, t,
    )
    mean_trace = trace[0, 0] / (rows * n)
    return out.reshape(tangent_blocks.shape), mean_trace


def solution(mesh):
    return jax.shard_map(
        body,
        mesh=mesh,
        in_specs=(
            P(AXES, None, None, None),
            P(AXES, None),
            P(AXES, None, None, None),
            P(AXES, None),
            P(AXES, None),
        ),
        out_specs=(P(AXES, None, None, None), P()),
        check_vma=False,
    )
```

```python
import functools

import jax
import jax.numpy as jnp
from jax import lax
from jax.experimental import pallas as pl
from jax.experimental.pallas import tpu as pltpu
from jax.sharding import PartitionSpec as P

HALF = 3
WIDTH = 2 * HALF + 1
WIN = 2 * HALF
AXES = ("row", "col")
VMEM_LIMIT = 58 * 1024 * 1024
F32 = jnp.float32
BF16 = jnp.bfloat16
I32 = jnp.int32


def need_cells(side):
    base = 0 if side == 0 else HALF
    return [
        (t, k, j)
        for t in range(2)
        for k in range(HALF)
        for j in range(WIN)
        if abs(j - (base + k)) <= HALF
    ]


def cell(t, k, j):
    return (t * HALF + k) * WIN + j


CELLS = 2 * HALF * WIN
RESULTS = HALF * WIN
CELL_ROW = (0, CELLS)
RESULT_ROW = (2 * CELLS, 2 * CELLS + RESULTS)
BIT_ROW = 2 * CELLS + 2 * RESULTS
COUNT_ROW = (BIT_ROW + WIN, BIT_ROW + WIN + 1)
LEFT_ROW = (BIT_ROW + WIN + 2, BIT_ROW + WIN + 3)
SUM_ROW = (BIT_ROW + WIN + 4, BIT_ROW + WIN + 5)
TOP_ROW = BIT_ROW + WIN + 6
PLAN_ROWS = 128


SECOND = 2


def split_room(room):
    last = room // 2
    return room - SECOND - last, SECOND, last


def either(flags):
    return functools.reduce(jnp.bitwise_or, flags)


def plan_kernel(slots, me_ref, meta_ref, out_ref, table):
    n = meta_ref.shape[-1]
    fields = 3 * slots

    def row(i, f):
        source, r = (0, i) if i < HALF else (1, i - HALF)
        at = r * fields + f
        return meta_ref[source, at : at + 1, :]

    one = jnp.ones((1, n), I32)
    zero = jnp.zeros((1, n), I32)
    live = [{}, {}]
    kept, shown = {}, {}
    for i in range(WIN):
        offs = [row(i, 2 * slots + s) for s in range(slots)]
        flags = [[jnp.where(row(i, t * slots + s) == 1, one, zero) for s in range(slots)] for t in range(2)]
        for j in range(WIN):
            d = j - i
            if abs(d) > HALF:
                continue
            here = [jnp.where(o == d, one, zero) for o in offs]
            kept[i, j] = either(here)
            shown[i, j] = one if d == 0 else kept[i, j]
            for t in range(2):
                live[t][i, j] = either([h & f for h, f in zip(here, flags[t])])

    def near(*pairs):
        return all(abs(p - q) <= HALF for p, q in pairs)

    as_left = {}
    for side in range(2):
        base, other = (0, HALF) if side == 0 else (HALF, 0)
        for t, k, j in need_cells(side):
            if other <= j < other + HALF:
                ends = [
                    live[1 - t][j, e] & shown[base + k, e] for e in range(WIN) if near((e, j), (e, base + k))
                ]
                as_left[side, t, k, j] = live[t][base + k, j] & either(ends)
    sums = {}
    for side in range(2):
        base, other = (0, HALF) if side == 0 else (HALF, 0)
        for i in range(other, other + HALF):
            for j in range(WIN):
                if near((i, j)):
                    terms = [
                        live[t][i, k] & live[1 - t][k, j]
                        for t in range(2)
                        for k in range(base, base + HALF)
                        if near((i, k), (k, j))
                    ]
                    if terms:
                        sums[side, i, j] = kept[i, j] & either(terms)

    def visit(bits, on_left, on_cell, on_sum):
        for side in range(2):
            base, other = (0, HALF) if side == 0 else (HALF, 0)

            def is_cross(spec):
                return other <= spec[2] < other + HALF

            lefts = {}
            for spec in need_cells(side):
                if is_cross(spec):
                    t, k, j = spec
                    lefts[spec] = bits[base + k] & as_left[side, t, k, j]
                    on_left(side, spec, lefts[spec])
            for spec in sorted(need_cells(side), key=lambda c: not is_cross(c)):
                t, k, j = spec
                kk = base + k
                users = [
                    live[1 - t][i, kk] & shown[i, j] & (1 - bits[i])
                    for i in range(other, other + HALF)
                    if near((i, kk), (i, j))
                ]
                need = either(users) & live[t][kk, j]
                if spec in lefts:
                    need = need & (1 - lefts[spec])
                on_cell(side, spec, is_cross(spec), need, lefts.get(spec))
            for i in range(other, other + HALF):
                for j in range(WIN):
                    if (side, i, j) in sums:
                        on_sum(side, i - other, j, sums[side, i, j] & bits[i])

    trials = 2**WIN
    trial = lax.broadcasted_iota(I32, (trials, n), 0)
    totals = {}

    def tally(name, side, value):
        totals[name, side] = totals[name, side] + value if (name, side) in totals else value

    def count_left(side, spec, need):
        for name in ("all", "cross", "left"):
            tally(name, side, need)

    def count_cell(side, spec, cross, need, left):
        tally("all", side, need)
        if cross:
            tally("cross", side, need)

    visit(
        [(trial >> i) & 1 for i in range(WIN)],
        count_left,
        count_cell,
        lambda side, i, j, need: tally("sum", side, need),
    )
    cost = jnp.zeros((trials, n), I32)
    load = jnp.zeros((trials, n), I32)
    for side in range(2):
        both = totals["all", side] + totals["sum", side]
        load = load + both
        cost = jnp.maximum(cost, both)
        cost = jnp.maximum(cost, 2 * totals["cross", side] - 1)
        cost = jnp.maximum(cost, 2 * totals["sum", side])
        cost = jnp.maximum(cost, 2 * (totals["left", side] + SECOND) - 1)
    score = ((cost * 256 + load) * trials + trial).astype(F32)
    best = jnp.min(score, axis=0, keepdims=True)
    best = best.astype(I32)
    bits = [(best >> i) & 1 for i in range(WIN)]
    top = jnp.max((best >> (8 + WIN)).astype(F32), axis=1, keepdims=True).astype(I32)

    table[...] = jnp.full(table.shape, -1, I32)

    def put(at, value):
        table[at : at + 1, :] = value

    counts = {key: zero for key in [(name, side) for name in ("all", "left", "sum") for side in range(2)]}

    left_places = {}

    def place_left(side, spec, need):
        left_places[side, spec] = jnp.where(need == 1, counts["all", side], -one)
        for name in ("all", "left"):
            counts[name, side] = counts[name, side] + need

    def place_cell(side, spec, cross, need, left):
        place = left_places.get((side, spec), -one)
        put(CELL_ROW[side] + cell(*spec), jnp.where(need == 1, counts["all", side], place))
        counts["all", side] = counts["all", side] + need

    def place_sum(side, i, j, need):
        put(RESULT_ROW[side] + i * WIN + j, jnp.where(need == 1, counts["sum", side], -one))
        counts["sum", side] = counts["sum", side] + need

    visit(bits, place_left, place_cell, place_sum)
    for i in range(WIN):
        put(BIT_ROW + i, bits[i])
    for side in range(2):
        put(COUNT_ROW[side], counts["all", side])
        put(LEFT_ROW[side], counts["left", side])
        put(SUM_ROW[side], counts["sum", side])
    put(TOP_ROW, jnp.broadcast_to(top, (1, n)))

    me = me_ref[0]
    whole = table[...]
    lane = lax.broadcasted_iota(I32, whole.shape, 1)
    right = lax.rem(me + 1, n)
    first = jnp.sum(jnp.where(lane == me, whole, 0), axis=1, keepdims=True)
    second = jnp.sum(jnp.where(lane == right, whole, 0), axis=1, keepdims=True)
    out_lane = lax.broadcasted_iota(I32, out_ref.shape, 1)
    out_ref[...] = jnp.where(out_lane == 0, first, second)


def make_plan(meta, me, slots):
    n, rows = meta.shape[0], meta.shape[1]
    low = jnp.roll(meta[:, rows - HALF :], 1, axis=0).reshape(n, -1).T
    high = meta[:, :HALF].reshape(n, -1).T
    return pl.pallas_call(
        functools.partial(plan_kernel, slots),
        out_shape=jax.ShapeDtypeStruct((PLAN_ROWS, 128), I32),
        in_specs=[pl.BlockSpec(memory_space=pltpu.SMEM), pl.BlockSpec(memory_space=pltpu.VMEM)],
        out_specs=pl.BlockSpec(memory_space=pltpu.VMEM),
        scratch_shapes=[pltpu.VMEM((PLAN_ROWS, n), I32)],
        name="plan",
    )(me.reshape(1), jnp.stack([low, high]))


SMEM = pl.BlockSpec(memory_space=pltpu.SMEM)
VMEM = pl.BlockSpec(memory_space=pltpu.VMEM)
HBM = pl.BlockSpec(memory_space=pl.ANY)
SENT = 2 * HALF * WIN + 1


def over(count, act, begin=0):
    def step(i, carry):
        act(i)
        return carry

    lax.fori_loop(begin, count, step, 0)


def list_sent(rows, own_ref, left_ref, right_ref, sent_ref):
    for side, plan_ref in ((0, right_ref), (1, left_ref)):
        for t, k, j in need_cells(side):
            own_row = rows - HALF + k if side == 0 else k
            place = j - k + HALF if side == 0 else j - k
            at = plan_ref[CELL_ROW[side] + cell(t, k, j)]
            at = jnp.where(at >= 0, at, SENT - 1)
            sent_ref[side * SENT + at] = own_ref[(t * rows + own_row) * WIDTH + place]


class Carrier:
    def __init__(self, side, low, high, shift, sent_ref, x_ref, t_ref, out, held, sems_in, sems_out):
        self.side, self.low, self.count, self.shift = side, low, jnp.maximum(high - low, 0), shift
        self.sent_ref, self.sources, self.out, self.held = sent_ref, (x_ref, t_ref), out, held
        self.sems_in, self.sems_out = sems_in, sems_out

    def arrival(self, t, block, i):
        return pltpu.make_async_copy(self.sources[t].at[block], self.held.at[self.side, i], self.sems_in.at[self.side, i])

    def departure(self, i):
        target = self.out.at[self.shift + i]
        return pltpu.make_async_copy(self.held.at[self.side, i], target, self.sems_out.at[self.side, i])

    def begin(self):
        stored = self.sources[0].shape[0]

        def act(i):
            block = self.sent_ref[self.side * SENT + self.low + i]
            for t in range(2):

                @pl.when((block >= stored) == (t == 1))
                def _():
                    self.arrival(t, block - t * stored, i).start()

        over(self.count, act)

    def onward(self):
        def act(i):
            self.arrival(0, 0, i).wait()
            self.departure(i).start()

        over(self.count, act)

    def end(self):
        over(self.count, lambda i: self.departure(i).wait())


def pack_kernel(rows, low, high, own_ref, left_ref, right_ref, x_ref, t_ref, forth_out, back_out, sent_ref, held, sems_in, sems_out):
    list_sent(rows, own_ref, left_ref, right_ref, sent_ref)
    carriers = [
        Carrier(side, low, jnp.minimum(count, high), 0, sent_ref, x_ref, t_ref, out, held, sems_in, sems_out)
        for side, count, out in (
            (0, right_ref[COUNT_ROW[0]], forth_out),
            (1, left_ref[COUNT_ROW[1]], back_out),
        )
    ]
    for carrier in carriers:
        carrier.begin()
    for carrier in carriers:
        carrier.onward()
    for carrier in carriers:
        carrier.end()


def pack(own, left, right, x, t, low, high, rows):
    block = x.shape[1:]
    room = high - low
    shape = jax.ShapeDtypeStruct((room,) + block, F32)
    return pl.pallas_call(
        functools.partial(pack_kernel, rows, low, high),
        out_shape=(shape, shape, jax.ShapeDtypeStruct((2 * SENT,), I32)),
        in_specs=[SMEM] * 3 + [HBM] * 2,
        out_specs=(HBM, HBM, SMEM),
        scratch_shapes=[
            pltpu.VMEM((2, room) + block, F32),
            pltpu.SemaphoreType.DMA((2, room)),
            pltpu.SemaphoreType.DMA((2, room)),
        ],
        compiler_params=pltpu.CompilerParams(vmem_limit_bytes=VMEM_LIMIT),
        name="pack",
    )(own, left, right, x, t)


def halves(values):
    high = values.astype(BF16)
    return high, (values - high.astype(F32)).astype(BF16)


STRIPE = 32


def stripes(block, act):
    over(block[0] // STRIPE, lambda i: act(pl.ds(pl.multiple_of(i * STRIPE, STRIPE), STRIPE)))


def split_block(source, at, high_ref, low_ref, to):
    def act(part):
        high_ref[to, part, :], low_ref[to, part, :] = halves(source[at, part, :])

    stripes(source.shape[1:], act)


def add_product(total, at, sign, lh, ll, i, rh, rl, j):
    dot = functools.partial(jnp.dot, preferred_element_type=F32)
    half = total.shape[-2] // 2

    def act(h):
        part = pl.ds(pl.multiple_of(h * half, half), half)
        high, low = lh[i, part, :], ll[i, part, :]
        result = dot(high, rh[j]) + (dot(high, rl[j]) + dot(low, rh[j]))
        total[at, part, :] += result if sign == 1 else sign * result

    over(2, act)


OWN, FIRST, LAST, HELP = range(4)
LEFT, RIGHT, BEGIN = range(3)


def list_length(rows, slots):
    return -(-((rows * slots + rows) * 2 * WIDTH + 1) // 128) * 128


def own_kernel(
    rows, slots, room_a, room_c, room_b,
    own_ref, left_ref, right_ref, off_ref, x_ref, t_ref,
    part_ref, high_ref, low_ref, lists_ref, used_ref,
):
    stored = rows * slots
    outs = stored + rows
    early = room_a + room_c
    late = [left_ref[SUM_ROW[0]] - early, room_b + right_ref[SUM_ROW[1]] - early]

    def clear(i, carry):
        used_ref[i] = 0
        return carry

    lax.fori_loop(0, 2 * stored, clear, 0)

    def of_output(q, counts):
        is_diag = q >= stored
        row = jnp.where(is_diag, q - stored, lax.div(q, slots))
        d = jnp.where(is_diag, 0, off_ref[jnp.minimum(q, stored - 1)])
        has_zero = jnp.bool_(False)
        for s in range(slots):
            has_zero = has_zero | (off_ref[row * slots + s] == 0)
        wanted = jnp.logical_not(is_diag & has_zero)
        for which in (OWN, FIRST, LAST):
            lists_ref[which, BEGIN, q] = counts[which]
        low_row = row - (rows - HALF)
        left_open = (row < HALF) & (left_ref[BIT_ROW + HALF + jnp.minimum(row, HALF - 1)] == 0)
        right_open = (low_row >= 0) & (right_ref[BIT_ROW + jnp.maximum(low_row, 0)] == 0)
        column = row + d

        def of_term(m, counts):
            t = lax.rem(m, 2)
            e = lax.div(m, 2) - HALF
            k = row + e
            place = d - e + HALF
            ok = wanted & (place >= 0) & (place < WIDTH)
            left = own_ref[(t * rows + row) * WIDTH + e + HALF]
            ok = ok & (left >= 0)
            is_own = ok & (k >= 0) & (k < rows)
            is_low = ok & (k < 0) & left_open
            is_high = ok & (k >= rows) & right_open
            own_block = own_ref[jnp.where(is_own, ((1 - t) * rows + k) * WIDTH + place, 0)]
            low_at = ((1 - t) * HALF + k + HALF) * WIN + column + HALF
            low_block = left_ref[CELL_ROW[0] + jnp.where(is_low, low_at, 0)]
            high_at = ((1 - t) * HALF + k - rows) * WIN + column - rows + HALF
            high_block = right_ref[CELL_ROW[1] + jnp.where(is_high, high_at, 0)]
            far_block = jnp.where(is_low, low_block, high_block)
            far_ok = (is_low | is_high) & (far_block >= 0)
            own_count, first_count, last_count = counts
            lists_ref[OWN, LEFT, own_count] = left
            lists_ref[OWN, RIGHT, own_count] = own_block
            own_count = own_count + jnp.where(is_own & (own_block >= 0), 1, 0)
            lists_ref[FIRST, LEFT, first_count] = left
            lists_ref[FIRST, RIGHT, first_count] = far_block + jnp.where(is_low, 0, early)
            first_count = first_count + jnp.where(far_ok & (far_block < early), 1, 0)
            lists_ref[LAST, LEFT, last_count] = left
            lists_ref[LAST, RIGHT, last_count] = far_block + jnp.where(is_low, late[0], late[1])
            is_last = far_ok & (far_block >= early)
            last_count = last_count + jnp.where(is_last, 1, 0)

            @pl.when(is_last)
            def _():
                used_ref[left] = 1

            return own_count, first_count, last_count

        return lax.fori_loop(0, 2 * WIDTH, of_term, counts)

    ends = lax.fori_loop(0, outs, of_output, (jnp.int32(0),) * 3)
    for which in (OWN, FIRST, LAST):
        lists_ref[which, BEGIN, outs] = ends[which]

    count = jnp.int32(0)
    for side, plan_ref in ((0, right_ref), (1, left_ref)):
        base, other = (0, HALF) if side == 0 else (HALF, 0)
        shift = rows - HALF if side == 0 else 0

        def of_sum(q, count):
            i = lax.div(q, WIN)
            j = lax.rem(q, WIN)
            open_row = plan_ref[BIT_ROW + other + i] == 1
            shown = (plan_ref[RESULT_ROW[side] + q] >= 0) | (j == other + i)
            open_row = open_row & shown
            lists_ref[HELP, BEGIN, side * RESULTS + q] = count

            def of_term(m, count):
                t = lax.rem(m, 2)
                k = lax.div(m, 2)
                reach = j - (base + k)
                ok = open_row & (reach >= -HALF) & (reach <= HALF)
                across = other + i - (base + k)
                ok = ok & (across >= -HALF) & (across <= HALF)
                left = plan_ref[CELL_ROW[1 - side] + (t * HALF + i) * WIN + base + k]
                right_at = jnp.where(ok, ((1 - t) * rows + shift + k) * WIDTH + reach + HALF, 0)
                right = own_ref[right_at]
                lists_ref[HELP, LEFT, count] = left + (room_a if side == 0 else 0)
                lists_ref[HELP, RIGHT, count] = right
                return count + jnp.where(ok & (left >= 0) & (right >= 0), 1, 0)

            return lax.fori_loop(0, 2 * HALF, of_term, count)

        count = lax.fori_loop(0, RESULTS, of_sum, count)
    lists_ref[HELP, BEGIN, 2 * RESULTS] = count

    def split(i, carry):
        for t, source in enumerate((x_ref, t_ref)):
            split_block(source, i, high_ref, low_ref, t * stored + i)
        return carry

    lax.fori_loop(0, stored, split, 0)

    def compute(q, carry):
        part_ref[q] = jnp.zeros(part_ref.shape[1:], F32)

        def term(m, carry):
            left = lists_ref[OWN, LEFT, m]
            right = lists_ref[OWN, RIGHT, m]
            add_product(part_ref, q, 1, high_ref, low_ref, left, high_ref, low_ref, right)
            return carry

        return lax.fori_loop(lists_ref[OWN, BEGIN, q], lists_ref[OWN, BEGIN, q + 1], term, carry)

    lax.fori_loop(0, outs, compute, 0)


def own_part(own, left, right, offsets, x, t, room_a, room_c, room_b, rows, slots):
    stored = rows * slots
    block = x.shape[1:]
    length = list_length(rows, slots)
    return pl.pallas_call(
        functools.partial(own_kernel, rows, slots, room_a, room_c, room_b),
        out_shape=(
            jax.ShapeDtypeStruct((stored + rows,) + block, F32),
            jax.ShapeDtypeStruct((2 * stored,) + block, BF16),
            jax.ShapeDtypeStruct((2 * stored,) + block, BF16),
            jax.ShapeDtypeStruct((4, 3, length), I32),
            jax.ShapeDtypeStruct((2 * stored,), I32),
        ),
        in_specs=[SMEM] * 4 + [VMEM] * 2,
        out_specs=(VMEM, VMEM, VMEM, SMEM, SMEM),
        compiler_params=pltpu.CompilerParams(vmem_limit_bytes=VMEM_LIMIT),
        cost_estimate=pl.CostEstimate(
            flops=2**20, bytes_accessed=2**16, transcendentals=0
        ),
        name="own_rows",
    )(own, left, right, offsets, x, t)


def convert_blocks(source, count, shift, far_high, far_low, stage, stage_sems):
    depth = stage.shape[0]

    def fetch(i):
        slot = lax.rem(i, depth)
        return pltpu.make_async_copy(source.at[i], stage.at[slot], stage_sems.at[slot])

    for i in range(depth - 1):

        @pl.when(i < count)
        def _():
            fetch(i).start()

    def convert(i, carry):
        @pl.when(i + depth - 1 < count)
        def _():
            fetch(i + depth - 1).start()

        fetch(i).wait()
        split_block(stage, lax.rem(i, depth), far_high, far_low, shift + i)
        return carry

    lax.fori_loop(0, count, convert, 0)


def trace_of(ref, at):
    side = ref.shape[-1]

    def stripe(i, total):
        first = pl.multiple_of(i * STRIPE, STRIPE)
        row = lax.broadcasted_iota(I32, (STRIPE, side), 0) + first
        column = lax.broadcasted_iota(I32, (STRIPE, side), 1)
        return total + jnp.where(row == column, ref[at, pl.ds(first, STRIPE), :], 0.0)

    return jnp.sum(lax.fori_loop(0, side // STRIPE, stripe, jnp.zeros((STRIPE, side), F32)))


def help_kernel(
    rows, room_a, early, room_b,
    sent_ref, left_ref, right_ref, lists_ref,
    low_ref, high_ref, own_high_ref, own_low_ref, x_ref, t_ref,
    forth_out, back_out, trace_ref,
    stage, far_high, far_low, own_high, own_low, sums, held, stage_sems, sems, sum_sems, sems_in, sems_out,
):
    outs = (forth_out, back_out)
    copies = [
        pltpu.make_async_copy(source, target, sems.at[i])
        for i, (source, target) in enumerate(((own_high_ref, own_high), (own_low_ref, own_low)))
    ]
    helps = lists_ref[HELP, BEGIN, 2 * RESULTS] > 0

    @pl.when(helps)
    def _():
        for copy in copies:
            copy.start()

    shifts = (right_ref[SUM_ROW[0]], left_ref[SUM_ROW[1]])
    carriers = [
        Carrier(side, early, count, shifts[side], sent_ref, x_ref, t_ref, outs[side], held, sems_in, sems_out)
        for side, count in ((0, right_ref[COUNT_ROW[0]]), (1, left_ref[COUNT_ROW[1]]))
    ]
    for carrier in carriers:
        carrier.begin()
    trace_ref[0, 0] = jnp.float32(0)

    @pl.when(helps)
    def _():
        convert_blocks(low_ref, left_ref[LEFT_ROW[0]], 0, far_high, far_low, stage, stage_sems)
        convert_blocks(high_ref, right_ref[LEFT_ROW[1]], room_a, far_high, far_low, stage, stage_sems)
        for copy in copies:
            copy.wait()

    for carrier in carriers:
        carrier.onward()
    for side, plan_ref in ((0, right_ref), (1, left_ref)):
        other = HALF if side == 0 else 0

        def compute(q, carry):
            begin_at = lists_ref[HELP, BEGIN, side * RESULTS + q]
            end_at = lists_ref[HELP, BEGIN, side * RESULTS + q + 1]
            at = plan_ref[RESULT_ROW[side] + q]

            @pl.when(end_at > begin_at)
            def _():
                slot = jnp.where(at >= 0, at, room_b)
                sums[side, slot] = jnp.zeros(sums.shape[2:], F32)

                def term(m, carry):
                    left = lists_ref[HELP, LEFT, m]
                    right = lists_ref[HELP, RIGHT, m]
                    add_product(sums.at[side], slot, 1, far_high, far_low, left, own_high, own_low, right)
                    return carry

                lax.fori_loop(begin_at, end_at, term, 0)

                @pl.when(at >= 0)
                def _():
                    pltpu.make_async_copy(sums.at[side, slot], outs[side].at[slot], sum_sems.at[side, slot]).start()

                @pl.when(lax.rem(q, WIN) == other + lax.div(q, WIN))
                def _():
                    trace_ref[0, 0] += trace_of(sums.at[side], slot)

            return carry

        lax.fori_loop(0, RESULTS, compute, 0)
    for side in range(2):

        def finish(i, carry):
            pltpu.make_async_copy(sums.at[side, i], outs[side].at[i], sum_sems.at[side, i]).wait()
            return carry

        lax.fori_loop(0, shifts[side], finish, 0)
    for carrier in carriers:
        carrier.end()


def help_part(sent, left, right, lists, low, high, own_high, own_low, x, t, early, room_b, rows):
    room_a = low.shape[0]
    block = x.shape[1:]
    stored = x.shape[0]
    shape = jax.ShapeDtypeStruct((room_b,) + block, F32)
    return pl.pallas_call(
        functools.partial(help_kernel, rows, room_a, early, room_b),
        out_shape=(shape, shape, jax.ShapeDtypeStruct((1, 1), F32)),
        in_specs=[SMEM] * 4 + [HBM] * 6,
        out_specs=(HBM, HBM, SMEM),
        scratch_shapes=[
            pltpu.VMEM((4,) + block, F32),
            pltpu.VMEM((2 * room_a,) + block, BF16),
            pltpu.VMEM((2 * room_a,) + block, BF16),
            pltpu.VMEM((2 * stored,) + block, BF16),
            pltpu.VMEM((2 * stored,) + block, BF16),
            pltpu.VMEM((2, room_b + 1) + block, F32),
            pltpu.VMEM((2, room_b) + block, F32),
            pltpu.SemaphoreType.DMA((4,)),
            pltpu.SemaphoreType.DMA((2,)),
            pltpu.SemaphoreType.DMA((2, room_b)),
            pltpu.SemaphoreType.DMA((2, room_b)),
            pltpu.SemaphoreType.DMA((2, room_b)),
        ],
        compiler_params=pltpu.CompilerParams(vmem_limit_bytes=VMEM_LIMIT),
        cost_estimate=pl.CostEstimate(
            flops=2**20, bytes_accessed=2**16, transcendentals=0
        ),
        name="help_rows",
)(sent, left, right, lists, low, high, own_high, own_low, x, t)


def first_kernel(
    rows, slots, room_a, room_c,
    lists_ref, left_ref, right_ref, off_ref, weight_ref,
    low_ref, high_ref, low_ref_2, high_ref_2, own_high_ref, own_low_ref, part_ref, t_ref,
    out_ref, trace_ref,
    stage, far_high, far_low, own_high, own_low, total, tangent, stage_sems, sems,
):
    stored = rows * slots
    outs = stored + rows
    copies = [
        pltpu.make_async_copy(source, target, sems.at[i])
        for i, (source, target) in enumerate(
            ((own_high_ref, own_high), (own_low_ref, own_low), (part_ref, total), (t_ref, tangent))
        )
    ]
    for copy in copies:
        copy.start()
    early = room_a + room_c
    for side, (source, source_2, plan_ref) in enumerate(
        ((low_ref, low_ref_2, left_ref), (high_ref, high_ref_2, right_ref))
    ):
        whole = plan_ref[COUNT_ROW[side]]
        convert_blocks(source, jnp.minimum(whole, room_a), side * early, far_high, far_low, stage, stage_sems)
        count = jnp.maximum(jnp.minimum(whole, early) - room_a, 0)
        convert_blocks(source_2, count, side * early + room_a, far_high, far_low, stage, stage_sems)
    for copy in copies:
        copy.wait()

    trace_ref[0, 0] = jnp.float32(0)

    def compute(q, carry):
        def term(m, carry):
            left = lists_ref[FIRST, LEFT, m]
            right = lists_ref[FIRST, RIGHT, m]
            add_product(total, q, 1, own_high, own_low, left, far_high, far_low, right)
            return carry

        lax.fori_loop(lists_ref[FIRST, BEGIN, q], lists_ref[FIRST, BEGIN, q + 1], term, 0)

        @pl.when(q < stored)
        def _():
            at = jnp.minimum(q, stored - 1)
            scale = 1.5 * weight_ref[at].astype(F32)

            def act(part):
                out_ref[at, part, :] = scale * tangent[at, part, :] - 0.5 * total[q, part, :]

            stripes(total.shape[1:], act)

        @pl.when((q >= stored) | (off_ref[jnp.minimum(q, stored - 1)] == 0))
        def _():
            trace_ref[0, 0] += trace_of(total, q)

        return carry

    lax.fori_loop(0, outs, compute, 0)


def first_part(lists, left, right, offsets, weights, low, high, low_2, high_2, own_high, own_low, part, t, rows, slots):
    room_a, room_c = low.shape[0], low_2.shape[0]
    room = room_a + room_c
    stored = rows * slots
    block = t.shape[1:]
    return pl.pallas_call(
        functools.partial(first_kernel, rows, slots, room_a, room_c),
        out_shape=(
            jax.ShapeDtypeStruct((stored,) + block, F32),
            jax.ShapeDtypeStruct((1, 1), F32),
        ),
        in_specs=[SMEM] * 5 + [HBM] * 8,
        out_specs=(VMEM, SMEM),
        scratch_shapes=[
            pltpu.VMEM((4,) + block, F32),
            pltpu.VMEM((2 * room,) + block, BF16),
            pltpu.VMEM((2 * room,) + block, BF16),
            pltpu.VMEM((2 * stored,) + block, BF16),
            pltpu.VMEM((2 * stored,) + block, BF16),
            pltpu.VMEM((stored + rows,) + block, F32),
            pltpu.VMEM((stored,) + block, F32),
            pltpu.SemaphoreType.DMA((4,)),
            pltpu.SemaphoreType.DMA((4,)),
        ],
        compiler_params=pltpu.CompilerParams(vmem_limit_bytes=VMEM_LIMIT),
        cost_estimate=pl.CostEstimate(
            flops=2**20, bytes_accessed=2**16, transcendentals=0
        ),
        name="first_halo",
    )(lists, left, right, offsets, weights, low, high, low_2, high_2, own_high, own_low, part, t)


def last_kernel(
    rows, slots, early, room_b,
    lists_ref, used_ref, left_ref, right_ref, off_ref,
    low_ref, high_ref, own_high_ref, own_low_ref, given_ref,
    out_ref,
    got, far_high, far_low, own_high, own_low, held, got_sems, own_sems, in_sems, out_sems,
):
    stored = rows * slots
    plans = (left_ref, right_ref)
    sources = (low_ref, high_ref)
    sum_counts = [plans[side][SUM_ROW[side]] for side in range(2)]
    counts = [
        sum_counts[side] + jnp.maximum(plans[side][COUNT_ROW[side]] - early, 0) for side in range(2)
    ]

    def fetch(side, i):
        return pltpu.make_async_copy(sources[side].at[i], got.at[side, i], got_sems.at[side, i])

    def places(q):
        row = lax.div(q, slots)
        column = row + off_ref[q]
        low_ok = (row < HALF) & (column < HALF)
        low_at = left_ref[RESULT_ROW[0] + jnp.where(low_ok, row * WIN + column + HALF, 0)]
        low_at = jnp.where(low_ok, low_at, -1)
        base = rows - HALF
        high_ok = (row >= base) & (column >= base)
        high_at = right_ref[RESULT_ROW[1] + jnp.where(high_ok, (row - base) * WIN + column - base, 0)]
        high_at = jnp.where(high_ok, high_at, -1)
        begin, end = lists_ref[LAST, BEGIN, q], lists_ref[LAST, BEGIN, q + 1]
        return low_at, high_at, begin, end

    def touched(q):
        low_at, high_at, begin, end = places(q)
        return (low_at >= 0) | (high_at >= 0) | (end > begin)

    def load(q):
        return pltpu.make_async_copy(given_ref.at[q], held.at[q], in_sems.at[q])

    def store(q):
        return pltpu.make_async_copy(held.at[q], out_ref.at[q], out_sems.at[q])

    for side in range(2):
        over(counts[side], lambda i, side=side: fetch(side, i).start())

    def when_touched(act):
        def step(q):
            @pl.when(touched(q))
            def _():
                act(q)

        return step

    over(stored, when_touched(lambda q: load(q).start()))

    def own_copies(i):
        return (
            pltpu.make_async_copy(own_high_ref.at[i], own_high.at[i], own_sems.at[0, i]),
            pltpu.make_async_copy(own_low_ref.at[i], own_low.at[i], own_sems.at[1, i]),
        )

    def on_used(act):
        def step(i):
            @pl.when(used_ref[i] == 1)
            def _():
                for copy in own_copies(i):
                    act(copy)

        over(2 * stored, step)

    on_used(lambda copy: copy.start())
    for side in range(2):
        over(counts[side], lambda i, side=side: fetch(side, i).wait())

        def convert(i, carry):
            split_block(got.at[side], i, far_high, far_low, side * room_b + i)
            return carry

        lax.fori_loop(sum_counts[side], counts[side], convert, 0)
    on_used(lambda copy: copy.wait())

    def compute(q):
        low_at, high_at, begin, end = places(q)
        load(q).wait()

        @pl.when(low_at >= 0)
        def _():
            held[q] -= 0.5 * got[0, low_at]

        @pl.when(high_at >= 0)
        def _():
            held[q] -= 0.5 * got[1, high_at]

        def term(m, carry):
            left = lists_ref[LAST, LEFT, m]
            right = lists_ref[LAST, RIGHT, m]
            add_product(held, q, -0.5, own_high, own_low, left, far_high, far_low, right)
            return carry

        lax.fori_loop(begin, end, term, 0)
        store(q).start()

    over(stored, when_touched(compute))
    over(stored, when_touched(lambda q: store(q).wait()))


def last_part(lists, used, left, right, offsets, low, high, own_high, own_low, given, early, rows, slots):
    room_b = low.shape[0]
    stored = rows * slots
    block = given.shape[1:]
    return pl.pallas_call(
        functools.partial(last_kernel, rows, slots, early, room_b),
        out_shape=jax.ShapeDtypeStruct(given.shape, F32),
        in_specs=[SMEM] * 5 + [HBM] * 5,
        out_specs=HBM,
        input_output_aliases={9: 0},
        scratch_shapes=[
            pltpu.VMEM((2, room_b) + block, F32),
            pltpu.VMEM((2 * room_b,) + block, BF16),
            pltpu.VMEM((2 * room_b,) + block, BF16),
            pltpu.VMEM((2 * stored,) + block, BF16),
            pltpu.VMEM((2 * stored,) + block, BF16),
            pltpu.VMEM((stored,) + block, F32),
            pltpu.SemaphoreType.DMA((2, room_b)),
            pltpu.SemaphoreType.DMA((2, 2 * stored)),
            pltpu.SemaphoreType.DMA((stored,)),
            pltpu.SemaphoreType.DMA((stored,)),
        ],
        compiler_params=pltpu.CompilerParams(vmem_limit_bytes=VMEM_LIMIT),
        cost_estimate=pl.CostEstimate(
            flops=2**20, bytes_accessed=2**16, transcendentals=0
        ),
        name="last_halo",
    )(lists, used, left, right, offsets, low, high, own_high, own_low, given)


def partners(value, n, step):
    return lax.ppermute(value, AXES, [(i, i ^ step) for i in range(n)])


def steps_of(n):
    step = 1
    while step < n:
        yield (step, 2 * step, 3 * step) if 2 * step < n else (step,)
        step *= 4


def gather_all(value, n):
    if n & (n - 1):
        return lax.all_gather(value, AXES)
    value = value[None]
    for steps in steps_of(n):
        value = jnp.concatenate([value] + [partners(value, n, step) for step in steps])
    me = lax.axis_index(AXES)
    step = 1
    while step < n:
        pairs = value.reshape((n // (2 * step), 2, step) + value.shape[1:])
        value = jnp.where((me // step) % 2 == 0, pairs, pairs[:, ::-1]).reshape(value.shape)
        step *= 2
    return value


def sum_all(value, n, wait_for=None):
    if n & (n - 1):
        return lax.psum(value, AXES), wait_for
    step, count = 1, 0
    while step < n:
        if count == 2:
            value, wait_for = lax.optimization_barrier((value, wait_for))
        value = value + partners(value, n, step)
        step, count = 2 * step, count + 1
    return value, wait_for


def body(density_blocks, density_live, tangent_blocks, tangent_live, block_offsets):
    rows, slots = density_live.shape
    block = density_blocks.shape[2:]
    n = lax.axis_size("row") * lax.axis_size("col")
    me = lax.axis_index(AXES).astype(I32)
    x = density_blocks.reshape((rows * slots,) + block)
    t = tangent_blocks.reshape((rows * slots,) + block)
    offsets = block_offsets.reshape(-1)
    weights = tangent_live.reshape(-1)

    meta = jnp.concatenate([density_live, tangent_live, block_offsets], axis=1)
    gathered = gather_all(meta, n)
    plan = make_plan(gathered, me, slots)
    left, right = plan[:, 0], plan[:, 1]

    index = jnp.arange(rows * slots, dtype=I32).reshape(rows, slots, 1)
    here = block_offsets[:, :, None] == jnp.arange(-HALF, HALF + 1, dtype=I32)
    own = jnp.stack(
        [
            jnp.max(jnp.where(here & (live == 1)[:, :, None], index + shift, -1), axis=1)
            for live, shift in ((density_live, 0), (tangent_live, rows * slots))
        ]
    ).reshape(-1)

    forward = [(i, (i + 1) % n) for i in range(n)]
    backward = [(b, a) for a, b in forward]

    def exchange(forth, back):
        return lax.ppermute(forth, AXES, forward), lax.ppermute(back, AXES, backward)

    def with_room(room, own, left, right, offsets, weights, x, t):
        room_a, room_c, room_b = split_room(room)
        early = room_a + room_c
        forth, back, sent = pack(own, left, right, x, t, 0, room_a, rows)
        low, high = exchange(forth, back)
        forth, back, _ = pack(own, left, right, x, t, room_a, early, rows)
        low_2, high_2 = exchange(forth, back)
        own, _, _ = lax.optimization_barrier((own, forth, back))
        part, own_high, own_low, lists, used = own_part(
            own, left, right, offsets, x, t, room_a, room_c, room_b, rows, slots
        )
        forth, back, help_trace = help_part(
            sent, left, right, lists, low, high, own_high, own_low, x, t, early, room_b, rows
        )
        forth, back, low_2, high_2 = lax.optimization_barrier((forth, back, low_2, high_2))
        last_low, last_high = exchange(forth, back)
        given, trace = first_part(
            lists, left, right, offsets, weights, low, high, low_2, high_2, own_high, own_low, part, t, rows, slots
        )
        out = last_part(
            lists, used, left, right, offsets, last_low, last_high, own_high, own_low, given, early, rows, slots
        )
        trace, out = sum_all(trace + help_trace, n, out)
        return out, trace

    worst = len(need_cells(0))
    rooms = [r for r in (15, 16, 17, 18, 19, 20, 22) if r < worst] + [worst]
    choice = jnp.sum((left[TOP_ROW] > jnp.array(rooms[:-1], I32)).astype(I32))
    out, trace = lax.switch(
        choice,
        [functools.partial(with_room, room) for room in rooms],
        own, left, right, offsets, weights, x, t,
    )
    mean_trace = trace[0, 0] / (rows * n)
    return out.reshape(tangent_blocks.shape), mean_trace


def solution(mesh):
    return jax.shard_map(
        body,
        mesh=mesh,
        in_specs=(
            P(AXES, None, None, None),
            P(AXES, None),
            P(AXES, None, None, None),
            P(AXES, None),
            P(AXES, None),
        ),
        out_specs=(P(AXES, None, None, None), P()),
        check_vma=False,
    )
```

```python
import functools

import jax
import jax.numpy as jnp
from jax import lax
from jax.experimental import pallas as pl
from jax.experimental.pallas import tpu as pltpu
from jax.sharding import PartitionSpec as P

HALF = 3
WIDTH = 2 * HALF + 1
WIN = 2 * HALF
AXES = ("row", "col")
VMEM_LIMIT = 58 * 1024 * 1024
F32 = jnp.float32
BF16 = jnp.bfloat16
I32 = jnp.int32


def need_cells(side):
    base = 0 if side == 0 else HALF
    return [
        (t, k, j)
        for t in range(2)
        for k in range(HALF)
        for j in range(WIN)
        if abs(j - (base + k)) <= HALF
    ]


def cell(t, k, j):
    return (t * HALF + k) * WIN + j


CELLS = 2 * HALF * WIN
RESULTS = HALF * WIN
CELL_ROW = (0, CELLS)
RESULT_ROW = (2 * CELLS, 2 * CELLS + RESULTS)
BIT_ROW = 2 * CELLS + 2 * RESULTS
COUNT_ROW = (BIT_ROW + WIN, BIT_ROW + WIN + 1)
LEFT_ROW = (BIT_ROW + WIN + 2, BIT_ROW + WIN + 3)
SUM_ROW = (BIT_ROW + WIN + 4, BIT_ROW + WIN + 5)
CHOICE_ROW = BIT_ROW + WIN + 6
PLAN_ROWS = 128


SECOND = 2


def split_room(room):
    last = room // 2
    return room - SECOND - last, SECOND, last


def either(flags):
    return functools.reduce(jnp.bitwise_or, flags)


def plan_kernel(slots, rooms, me_ref, meta_ref, out_ref, table):
    n = meta_ref.shape[-1]
    fields = 3 * slots

    def row(i, f):
        source, r = (0, i) if i < HALF else (1, i - HALF)
        at = r * fields + f
        return meta_ref[source, at : at + 1, :]

    one = jnp.ones((1, n), I32)
    zero = jnp.zeros((1, n), I32)
    live = [{}, {}]
    kept, shown = {}, {}
    for i in range(WIN):
        offs = [row(i, 2 * slots + s) for s in range(slots)]
        flags = [[jnp.where(row(i, t * slots + s) == 1, one, zero) for s in range(slots)] for t in range(2)]
        for j in range(WIN):
            d = j - i
            if abs(d) > HALF:
                continue
            here = [jnp.where(o == d, one, zero) for o in offs]
            kept[i, j] = either(here)
            shown[i, j] = one if d == 0 else kept[i, j]
            for t in range(2):
                live[t][i, j] = either([h & f for h, f in zip(here, flags[t])])

    def near(*pairs):
        return all(abs(p - q) <= HALF for p, q in pairs)

    as_left = {}
    for side in range(2):
        base, other = (0, HALF) if side == 0 else (HALF, 0)
        for t, k, j in need_cells(side):
            if other <= j < other + HALF:
                ends = [
                    live[1 - t][j, e] & shown[base + k, e] for e in range(WIN) if near((e, j), (e, base + k))
                ]
                as_left[side, t, k, j] = live[t][base + k, j] & either(ends)
    sums = {}
    for side in range(2):
        base, other = (0, HALF) if side == 0 else (HALF, 0)
        for i in range(other, other + HALF):
            for j in range(WIN):
                if near((i, j)):
                    terms = [
                        live[t][i, k] & live[1 - t][k, j]
                        for t in range(2)
                        for k in range(base, base + HALF)
                        if near((i, k), (k, j))
                    ]
                    if terms:
                        sums[side, i, j] = kept[i, j] & either(terms)

    def visit(bits, on_left, on_cell, on_sum):
        for side in range(2):
            base, other = (0, HALF) if side == 0 else (HALF, 0)

            def is_cross(spec):
                return other <= spec[2] < other + HALF

            lefts = {}
            for spec in need_cells(side):
                if is_cross(spec):
                    t, k, j = spec
                    lefts[spec] = bits[base + k] & as_left[side, t, k, j]
                    on_left(side, spec, lefts[spec])
            for spec in sorted(need_cells(side), key=lambda c: not is_cross(c)):
                t, k, j = spec
                kk = base + k
                users = [
                    live[1 - t][i, kk] & shown[i, j] & (1 - bits[i])
                    for i in range(other, other + HALF)
                    if near((i, kk), (i, j))
                ]
                need = either(users) & live[t][kk, j]
                if spec in lefts:
                    need = need & (1 - lefts[spec])
                on_cell(side, spec, is_cross(spec), need, lefts.get(spec))
            for i in range(other, other + HALF):
                for j in range(WIN):
                    if (side, i, j) in sums:
                        on_sum(side, i - other, j, sums[side, i, j] & bits[i])

    trials = 2**WIN
    trial = lax.broadcasted_iota(I32, (trials, n), 0)
    totals = {}

    def tally(name, side, value):
        totals[name, side] = totals[name, side] + value if (name, side) in totals else value

    def count_left(side, spec, need):
        for name in ("all", "cross", "left"):
            tally(name, side, need)

    def count_cell(side, spec, cross, need, left):
        tally("all", side, need)
        if cross:
            tally("cross", side, need)

    visit(
        [(trial >> i) & 1 for i in range(WIN)],
        count_left,
        count_cell,
        lambda side, i, j, need: tally("sum", side, need),
    )
    cost = jnp.zeros((trials, n), I32)
    load = jnp.zeros((trials, n), I32)
    for side in range(2):
        both = totals["all", side] + totals["sum", side]
        load = load + both
        cost = jnp.maximum(cost, both)
        cost = jnp.maximum(cost, 2 * totals["cross", side] - 1)
        cost = jnp.maximum(cost, 2 * totals["sum", side])
        cost = jnp.maximum(cost, 2 * (totals["left", side] + SECOND) - 1)
    score = ((cost * 256 + load) * trials + trial).astype(F32)
    best = jnp.min(score, axis=0, keepdims=True)
    best = best.astype(I32)
    bits = [(best >> i) & 1 for i in range(WIN)]
    top = jnp.max((best >> (8 + WIN)).astype(F32), axis=1, keepdims=True).astype(I32)

    table[...] = jnp.full(table.shape, -1, I32)

    def put(at, value):
        table[at : at + 1, :] = value

    counts = {key: zero for key in [(name, side) for name in ("all", "left", "sum") for side in range(2)]}

    left_places = {}

    def place_left(side, spec, need):
        left_places[side, spec] = jnp.where(need == 1, counts["all", side], -one)
        for name in ("all", "left"):
            counts[name, side] = counts[name, side] + need

    def place_cell(side, spec, cross, need, left):
        place = left_places.get((side, spec), -one)
        put(CELL_ROW[side] + cell(*spec), jnp.where(need == 1, counts["all", side], place))
        counts["all", side] = counts["all", side] + need

    def place_sum(side, i, j, need):
        put(RESULT_ROW[side] + i * WIN + j, jnp.where(need == 1, counts["sum", side], -one))
        counts["sum", side] = counts["sum", side] + need

    visit(bits, place_left, place_cell, place_sum)
    for i in range(WIN):
        put(BIT_ROW + i, bits[i])
    for side in range(2):
        put(COUNT_ROW[side], counts["all", side])
        put(LEFT_ROW[side], counts["left", side])
        put(SUM_ROW[side], counts["sum", side])
    choice = sum(jnp.where(top > room, 1, 0) for room in rooms[:-1])
    put(CHOICE_ROW, jnp.broadcast_to(choice, (1, n)))

    me = me_ref[0]
    whole = table[...]
    lane = lax.broadcasted_iota(I32, whole.shape, 1)
    right = lax.rem(me + 1, n)
    first = jnp.sum(jnp.where(lane == me, whole, 0), axis=1, keepdims=True)
    second = jnp.sum(jnp.where(lane == right, whole, 0), axis=1, keepdims=True)
    out_lane = lax.broadcasted_iota(I32, out_ref.shape, 1)
    out_ref[...] = jnp.where(out_lane == 0, first, second)


def make_plan(meta, me, slots, rooms):
    n, rows = meta.shape[0], meta.shape[1]
    low = jnp.roll(meta[:, rows - HALF :], 1, axis=0).reshape(n, -1).T
    high = meta[:, :HALF].reshape(n, -1).T
    return pl.pallas_call(
        functools.partial(plan_kernel, slots, rooms),
        out_shape=jax.ShapeDtypeStruct((PLAN_ROWS, 128), I32),
        in_specs=[pl.BlockSpec(memory_space=pltpu.SMEM), pl.BlockSpec(memory_space=pltpu.VMEM)],
        out_specs=pl.BlockSpec(memory_space=pltpu.VMEM),
        scratch_shapes=[pltpu.VMEM((PLAN_ROWS, n), I32)],
        name="plan",
    )(me.reshape(1), jnp.stack([low, high]))


SMEM = pl.BlockSpec(memory_space=pltpu.SMEM)
VMEM = pl.BlockSpec(memory_space=pltpu.VMEM)
HBM = pl.BlockSpec(memory_space=pl.ANY)
SENT = 2 * HALF * WIN + 1


def over(count, act, begin=0):
    def step(i, carry):
        act(i)
        return carry

    lax.fori_loop(begin, count, step, 0)


def list_sent(rows, own_ref, left_ref, right_ref, sent_ref):
    for side, plan_ref in ((0, right_ref), (1, left_ref)):
        for t, k, j in need_cells(side):
            own_row = rows - HALF + k if side == 0 else k
            place = j - k + HALF if side == 0 else j - k
            at = plan_ref[CELL_ROW[side] + cell(t, k, j)]
            at = jnp.where(at >= 0, at, SENT - 1)
            sent_ref[side * SENT + at] = own_ref[(t * rows + own_row) * WIDTH + place]


class Carrier:
    def __init__(self, side, low, high, shift, sent_ref, x_ref, t_ref, out, held, sems_in, sems_out):
        self.side, self.low, self.count, self.shift = side, low, jnp.maximum(high - low, 0), shift
        self.sent_ref, self.sources, self.out, self.held = sent_ref, (x_ref, t_ref), out, held
        self.sems_in, self.sems_out = sems_in, sems_out

    def arrival(self, t, block, i):
        return pltpu.make_async_copy(self.sources[t].at[block], self.held.at[self.side, i], self.sems_in.at[self.side, i])

    def departure(self, i):
        target = self.out.at[self.shift + i]
        return pltpu.make_async_copy(self.held.at[self.side, i], target, self.sems_out.at[self.side, i])

    def begin(self):
        stored = self.sources[0].shape[0]

        def act(i):
            block = self.sent_ref[self.side * SENT + self.low + i]
            for t in range(2):

                @pl.when((block >= stored) == (t == 1))
                def _():
                    self.arrival(t, block - t * stored, i).start()

        over(self.count, act)

    def onward(self):
        def act(i):
            self.arrival(0, 0, i).wait()
            self.departure(i).start()

        over(self.count, act)

    def end(self):
        over(self.count, lambda i: self.departure(i).wait())


def pack_kernel(rows, low, high, own_ref, left_ref, right_ref, x_ref, t_ref, forth_out, back_out, sent_ref, held, sems_in, sems_out):
    list_sent(rows, own_ref, left_ref, right_ref, sent_ref)
    carriers = [
        Carrier(side, low, jnp.minimum(count, high), 0, sent_ref, x_ref, t_ref, out, held, sems_in, sems_out)
        for side, count, out in (
            (0, right_ref[COUNT_ROW[0]], forth_out),
            (1, left_ref[COUNT_ROW[1]], back_out),
        )
    ]
    for carrier in carriers:
        carrier.begin()
    for carrier in carriers:
        carrier.onward()
    for carrier in carriers:
        carrier.end()


def pack(own, left, right, x, t, low, high, rows):
    block = x.shape[1:]
    room = high - low
    shape = jax.ShapeDtypeStruct((room,) + block, F32)
    return pl.pallas_call(
        functools.partial(pack_kernel, rows, low, high),
        out_shape=(shape, shape, jax.ShapeDtypeStruct((2 * SENT,), I32)),
        in_specs=[SMEM] * 3 + [HBM] * 2,
        out_specs=(HBM, HBM, SMEM),
        scratch_shapes=[
            pltpu.VMEM((2, room) + block, F32),
            pltpu.SemaphoreType.DMA((2, room)),
            pltpu.SemaphoreType.DMA((2, room)),
        ],
        compiler_params=pltpu.CompilerParams(vmem_limit_bytes=VMEM_LIMIT),
        name="pack",
    )(own, left, right, x, t)


def halves(values):
    high = values.astype(BF16)
    return high, (values - high.astype(F32)).astype(BF16)


STRIPE = 32


def stripes(block, act):
    over(block[0] // STRIPE, lambda i: act(pl.ds(pl.multiple_of(i * STRIPE, STRIPE), STRIPE)))


def split_block(source, at, high_ref, low_ref, to):
    def act(part):
        high_ref[to, part, :], low_ref[to, part, :] = halves(source[at, part, :])

    stripes(source.shape[1:], act)


def add_product(total, at, sign, lh, ll, i, rh, rl, j):
    dot = functools.partial(jnp.dot, preferred_element_type=F32)
    half = total.shape[-2] // 2

    def act(h):
        part = pl.ds(pl.multiple_of(h * half, half), half)
        high, low = lh[i, part, :], ll[i, part, :]
        result = dot(high, rh[j]) + (dot(high, rl[j]) + dot(low, rh[j]))
        total[at, part, :] += result if sign == 1 else sign * result

    over(2, act)


OWN, FIRST, LAST, HELP = range(4)
LEFT, RIGHT, BEGIN = range(3)
OF_OWN, OF_OUT, OF_LOW, OF_HIGH, OF_COUNT = range(5)


def list_length(rows, slots):
    return -(-((rows * slots + rows) * 2 * WIDTH + 1) // 128) * 128


def own_kernel(
    rows, slots, room_a, room_c, room_b,
    own_ref, left_ref, right_ref, off_ref, x_ref, t_ref,
    part_ref, high_ref, low_ref, lists_ref, used_ref, late_ref,
):
    stored = rows * slots
    outs = stored + rows
    early = room_a + room_c
    late = [left_ref[SUM_ROW[0]] - early, room_b + right_ref[SUM_ROW[1]] - early]

    def clear(i, carry):
        used_ref[i] = 0
        return carry

    lax.fori_loop(0, 2 * stored, clear, 0)

    def of_output(q, counts):
        is_diag = q >= stored
        row = jnp.where(is_diag, q - stored, lax.div(q, slots))
        d = jnp.where(is_diag, 0, off_ref[jnp.minimum(q, stored - 1)])
        has_zero = jnp.bool_(False)
        for s in range(slots):
            has_zero = has_zero | (off_ref[row * slots + s] == 0)
        wanted = jnp.logical_not(is_diag & has_zero)
        for which in (OWN, FIRST, LAST):
            lists_ref[which, BEGIN, q] = counts[which]
        low_row = row - (rows - HALF)
        left_open = (row < HALF) & (left_ref[BIT_ROW + HALF + jnp.minimum(row, HALF - 1)] == 0)
        right_open = (low_row >= 0) & (right_ref[BIT_ROW + jnp.maximum(low_row, 0)] == 0)
        column = row + d

        def of_term(m, counts):
            t = lax.rem(m, 2)
            e = lax.div(m, 2) - HALF
            k = row + e
            place = d - e + HALF
            ok = wanted & (place >= 0) & (place < WIDTH)
            left = own_ref[(t * rows + row) * WIDTH + e + HALF]
            ok = ok & (left >= 0)
            is_own = ok & (k >= 0) & (k < rows)
            is_low = ok & (k < 0) & left_open
            is_high = ok & (k >= rows) & right_open
            own_block = own_ref[jnp.where(is_own, ((1 - t) * rows + k) * WIDTH + place, 0)]
            low_at = ((1 - t) * HALF + k + HALF) * WIN + column + HALF
            low_block = left_ref[CELL_ROW[0] + jnp.where(is_low, low_at, 0)]
            high_at = ((1 - t) * HALF + k - rows) * WIN + column - rows + HALF
            high_block = right_ref[CELL_ROW[1] + jnp.where(is_high, high_at, 0)]
            far_block = jnp.where(is_low, low_block, high_block)
            far_ok = (is_low | is_high) & (far_block >= 0)
            own_count, first_count, last_count = counts
            lists_ref[OWN, LEFT, own_count] = left
            lists_ref[OWN, RIGHT, own_count] = own_block
            own_count = own_count + jnp.where(is_own & (own_block >= 0), 1, 0)
            lists_ref[FIRST, LEFT, first_count] = left
            lists_ref[FIRST, RIGHT, first_count] = far_block + jnp.where(is_low, 0, early)
            first_count = first_count + jnp.where(far_ok & (far_block < early), 1, 0)
            lists_ref[LAST, LEFT, last_count] = left
            lists_ref[LAST, RIGHT, last_count] = far_block + jnp.where(is_low, late[0], late[1])
            is_last = far_ok & (far_block >= early)
            last_count = last_count + jnp.where(is_last, 1, 0)

            @pl.when(is_last)
            def _():
                used_ref[left] = 1

            return own_count, first_count, last_count

        return lax.fori_loop(0, 2 * WIDTH, of_term, counts)

    ends = lax.fori_loop(0, outs, of_output, (jnp.int32(0),) * 3)
    for which in (OWN, FIRST, LAST):
        lists_ref[which, BEGIN, outs] = ends[which]

    def list_own(i, count):
        late_ref[OF_OWN, count] = i
        return count + used_ref[i]

    late_ref[OF_COUNT, 0] = lax.fori_loop(0, 2 * stored, list_own, jnp.int32(0))

    def list_out(q, count):
        row = lax.div(q, slots)
        column = row + off_ref[q]
        base = rows - HALF
        low_ok = (row < HALF) & (column < HALF)
        low_at = left_ref[RESULT_ROW[0] + jnp.where(low_ok, row * WIN + column + HALF, 0)]
        low_at = jnp.where(low_ok, low_at, -1)
        high_ok = (row >= base) & (column >= base)
        high_at = right_ref[RESULT_ROW[1] + jnp.where(high_ok, (row - base) * WIN + column - base, 0)]
        high_at = jnp.where(high_ok, high_at, -1)
        late_ref[OF_OUT, count] = q
        late_ref[OF_LOW, count] = low_at
        late_ref[OF_HIGH, count] = high_at
        more = lists_ref[LAST, BEGIN, q + 1] > lists_ref[LAST, BEGIN, q]
        return count + jnp.where((low_at >= 0) | (high_at >= 0) | more, 1, 0)

    late_ref[OF_COUNT, 1] = lax.fori_loop(0, stored, list_out, jnp.int32(0))

    count = jnp.int32(0)
    for side, plan_ref in ((0, right_ref), (1, left_ref)):
        base, other = (0, HALF) if side == 0 else (HALF, 0)
        shift = rows - HALF if side == 0 else 0

        def of_sum(q, count):
            i = lax.div(q, WIN)
            j = lax.rem(q, WIN)
            open_row = plan_ref[BIT_ROW + other + i] == 1
            shown = (plan_ref[RESULT_ROW[side] + q] >= 0) | (j == other + i)
            open_row = open_row & shown
            lists_ref[HELP, BEGIN, side * RESULTS + q] = count

            def of_term(m, count):
                t = lax.rem(m, 2)
                k = lax.div(m, 2)
                reach = j - (base + k)
                ok = open_row & (reach >= -HALF) & (reach <= HALF)
                across = other + i - (base + k)
                ok = ok & (across >= -HALF) & (across <= HALF)
                left = plan_ref[CELL_ROW[1 - side] + (t * HALF + i) * WIN + base + k]
                right_at = jnp.where(ok, ((1 - t) * rows + shift + k) * WIDTH + reach + HALF, 0)
                right = own_ref[right_at]
                lists_ref[HELP, LEFT, count] = left + (room_a if side == 0 else 0)
                lists_ref[HELP, RIGHT, count] = right
                return count + jnp.where(ok & (left >= 0) & (right >= 0), 1, 0)

            return lax.fori_loop(0, 2 * HALF, of_term, count)

        count = lax.fori_loop(0, RESULTS, of_sum, count)
    lists_ref[HELP, BEGIN, 2 * RESULTS] = count

    def split(i, carry):
        for t, source in enumerate((x_ref, t_ref)):
            split_block(source, i, high_ref, low_ref, t * stored + i)
        return carry

    lax.fori_loop(0, stored, split, 0)

    def compute(q, carry):
        part_ref[q] = jnp.zeros(part_ref.shape[1:], F32)

        def term(m, carry):
            left = lists_ref[OWN, LEFT, m]
            right = lists_ref[OWN, RIGHT, m]
            add_product(part_ref, q, 1, high_ref, low_ref, left, high_ref, low_ref, right)
            return carry

        return lax.fori_loop(lists_ref[OWN, BEGIN, q], lists_ref[OWN, BEGIN, q + 1], term, carry)

    lax.fori_loop(0, outs, compute, 0)


def own_part(own, left, right, offsets, x, t, room_a, room_c, room_b, rows, slots):
    stored = rows * slots
    block = x.shape[1:]
    length = list_length(rows, slots)
    return pl.pallas_call(
        functools.partial(own_kernel, rows, slots, room_a, room_c, room_b),
        out_shape=(
            jax.ShapeDtypeStruct((stored + rows,) + block, F32),
            jax.ShapeDtypeStruct((2 * stored,) + block, BF16),
            jax.ShapeDtypeStruct((2 * stored,) + block, BF16),
            jax.ShapeDtypeStruct((4, 3, length), I32),
            jax.ShapeDtypeStruct((2 * stored,), I32),
            jax.ShapeDtypeStruct((5, 128), I32),
        ),
        in_specs=[SMEM] * 4 + [VMEM] * 2,
        out_specs=(VMEM, VMEM, VMEM, SMEM, SMEM, SMEM),
        compiler_params=pltpu.CompilerParams(vmem_limit_bytes=VMEM_LIMIT),
        cost_estimate=pl.CostEstimate(
            flops=2**20, bytes_accessed=2**16, transcendentals=0
        ),
        name="own_rows",
    )(own, left, right, offsets, x, t)


def convert_blocks(source, count, shift, far_high, far_low, stage, stage_sems):
    depth = stage.shape[0]

    def fetch(i):
        slot = lax.rem(i, depth)
        return pltpu.make_async_copy(source.at[i], stage.at[slot], stage_sems.at[slot])

    for i in range(depth - 1):

        @pl.when(i < count)
        def _():
            fetch(i).start()

    def convert(i, carry):
        @pl.when(i + depth - 1 < count)
        def _():
            fetch(i + depth - 1).start()

        fetch(i).wait()
        split_block(stage, lax.rem(i, depth), far_high, far_low, shift + i)
        return carry

    lax.fori_loop(0, count, convert, 0)


def trace_of(ref, at):
    side = ref.shape[-1]

    def stripe(i, total):
        first = pl.multiple_of(i * STRIPE, STRIPE)
        row = lax.broadcasted_iota(I32, (STRIPE, side), 0) + first
        column = lax.broadcasted_iota(I32, (STRIPE, side), 1)
        return total + jnp.where(row == column, ref[at, pl.ds(first, STRIPE), :], 0.0)

    return jnp.sum(lax.fori_loop(0, side // STRIPE, stripe, jnp.zeros((STRIPE, side), F32)))


def help_kernel(
    rows, room_a, early, room_b,
    sent_ref, left_ref, right_ref, lists_ref,
    low_ref, high_ref, own_high_ref, own_low_ref, x_ref, t_ref,
    forth_out, back_out, trace_ref,
    stage, far_high, far_low, own_high, own_low, sums, held, stage_sems, sems, sum_sems, sems_in, sems_out,
):
    outs = (forth_out, back_out)
    copies = [
        pltpu.make_async_copy(source, target, sems.at[i])
        for i, (source, target) in enumerate(((own_high_ref, own_high), (own_low_ref, own_low)))
    ]
    helps = lists_ref[HELP, BEGIN, 2 * RESULTS] > 0

    @pl.when(helps)
    def _():
        for copy in copies:
            copy.start()

    shifts = (right_ref[SUM_ROW[0]], left_ref[SUM_ROW[1]])
    carriers = [
        Carrier(side, early, count, shifts[side], sent_ref, x_ref, t_ref, outs[side], held, sems_in, sems_out)
        for side, count in ((0, right_ref[COUNT_ROW[0]]), (1, left_ref[COUNT_ROW[1]]))
    ]
    for carrier in carriers:
        carrier.begin()
    trace_ref[0, 0] = jnp.float32(0)

    @pl.when(helps)
    def _():
        convert_blocks(low_ref, left_ref[LEFT_ROW[0]], 0, far_high, far_low, stage, stage_sems)
        convert_blocks(high_ref, right_ref[LEFT_ROW[1]], room_a, far_high, far_low, stage, stage_sems)
        for copy in copies:
            copy.wait()

    for carrier in carriers:
        carrier.onward()
    for side, plan_ref in ((0, right_ref), (1, left_ref)):
        other = HALF if side == 0 else 0

        def compute(q, carry):
            begin_at = lists_ref[HELP, BEGIN, side * RESULTS + q]
            end_at = lists_ref[HELP, BEGIN, side * RESULTS + q + 1]
            at = plan_ref[RESULT_ROW[side] + q]

            @pl.when(end_at > begin_at)
            def _():
                slot = jnp.where(at >= 0, at, room_b)
                sums[side, slot] = jnp.zeros(sums.shape[2:], F32)

                def term(m, carry):
                    left = lists_ref[HELP, LEFT, m]
                    right = lists_ref[HELP, RIGHT, m]
                    add_product(sums.at[side], slot, 1, far_high, far_low, left, own_high, own_low, right)
                    return carry

                lax.fori_loop(begin_at, end_at, term, 0)

                @pl.when(at >= 0)
                def _():
                    pltpu.make_async_copy(sums.at[side, slot], outs[side].at[slot], sum_sems.at[side, slot]).start()

                @pl.when(lax.rem(q, WIN) == other + lax.div(q, WIN))
                def _():
                    trace_ref[0, 0] += trace_of(sums.at[side], slot)

            return carry

        lax.fori_loop(0, RESULTS, compute, 0)
    for side in range(2):

        def finish(i, carry):
            pltpu.make_async_copy(sums.at[side, i], outs[side].at[i], sum_sems.at[side, i]).wait()
            return carry

        lax.fori_loop(0, shifts[side], finish, 0)
    for carrier in carriers:
        carrier.end()


def help_part(sent, left, right, lists, low, high, own_high, own_low, x, t, early, room_b, rows):
    room_a = low.shape[0]
    block = x.shape[1:]
    stored = x.shape[0]
    shape = jax.ShapeDtypeStruct((room_b,) + block, F32)
    return pl.pallas_call(
        functools.partial(help_kernel, rows, room_a, early, room_b),
        out_shape=(shape, shape, jax.ShapeDtypeStruct((1, 1), F32)),
        in_specs=[SMEM] * 4 + [HBM] * 6,
        out_specs=(HBM, HBM, SMEM),
        scratch_shapes=[
            pltpu.VMEM((4,) + block, F32),
            pltpu.VMEM((2 * room_a,) + block, BF16),
            pltpu.VMEM((2 * room_a,) + block, BF16),
            pltpu.VMEM((2 * stored,) + block, BF16),
            pltpu.VMEM((2 * stored,) + block, BF16),
            pltpu.VMEM((2, room_b + 1) + block, F32),
            pltpu.VMEM((2, room_b) + block, F32),
            pltpu.SemaphoreType.DMA((4,)),
            pltpu.SemaphoreType.DMA((2,)),
            pltpu.SemaphoreType.DMA((2, room_b)),
            pltpu.SemaphoreType.DMA((2, room_b)),
            pltpu.SemaphoreType.DMA((2, room_b)),
        ],
        compiler_params=pltpu.CompilerParams(vmem_limit_bytes=VMEM_LIMIT),
        cost_estimate=pl.CostEstimate(
            flops=2**20, bytes_accessed=2**16, transcendentals=0
        ),
        name="help_rows",
)(sent, left, right, lists, low, high, own_high, own_low, x, t)


def first_kernel(
    rows, slots, room_a, room_c,
    lists_ref, left_ref, right_ref, off_ref, weight_ref,
    low_ref, high_ref, low_ref_2, high_ref_2, own_high_ref, own_low_ref, part_ref, t_ref,
    out_ref, trace_ref,
    stage, far_high, far_low, own_high, own_low, total, tangent, stage_sems, sems,
):
    stored = rows * slots
    outs = stored + rows
    copies = [
        pltpu.make_async_copy(source, target, sems.at[i])
        for i, (source, target) in enumerate(
            ((own_high_ref, own_high), (own_low_ref, own_low), (part_ref, total), (t_ref, tangent))
        )
    ]
    for copy in copies:
        copy.start()
    early = room_a + room_c
    for side, (source, source_2, plan_ref) in enumerate(
        ((low_ref, low_ref_2, left_ref), (high_ref, high_ref_2, right_ref))
    ):
        whole = plan_ref[COUNT_ROW[side]]
        convert_blocks(source, jnp.minimum(whole, room_a), side * early, far_high, far_low, stage, stage_sems)
        count = jnp.maximum(jnp.minimum(whole, early) - room_a, 0)
        convert_blocks(source_2, count, side * early + room_a, far_high, far_low, stage, stage_sems)
    for copy in copies:
        copy.wait()

    trace_ref[0, 0] = jnp.float32(0)

    def compute(q, carry):
        def term(m, carry):
            left = lists_ref[FIRST, LEFT, m]
            right = lists_ref[FIRST, RIGHT, m]
            add_product(total, q, 1, own_high, own_low, left, far_high, far_low, right)
            return carry

        lax.fori_loop(lists_ref[FIRST, BEGIN, q], lists_ref[FIRST, BEGIN, q + 1], term, 0)

        @pl.when(q < stored)
        def _():
            at = jnp.minimum(q, stored - 1)
            scale = 1.5 * weight_ref[at].astype(F32)

            def act(part):
                out_ref[at, part, :] = scale * tangent[at, part, :] - 0.5 * total[q, part, :]

            stripes(total.shape[1:], act)

        @pl.when((q >= stored) | (off_ref[jnp.minimum(q, stored - 1)] == 0))
        def _():
            trace_ref[0, 0] += trace_of(total, q)

        return carry

    lax.fori_loop(0, outs, compute, 0)


def first_part(lists, left, right, offsets, weights, low, high, low_2, high_2, own_high, own_low, part, t, rows, slots):
    room_a, room_c = low.shape[0], low_2.shape[0]
    room = room_a + room_c
    stored = rows * slots
    block = t.shape[1:]
    return pl.pallas_call(
        functools.partial(first_kernel, rows, slots, room_a, room_c),
        out_shape=(
            jax.ShapeDtypeStruct((stored,) + block, F32),
            jax.ShapeDtypeStruct((1, 1), F32),
        ),
        in_specs=[SMEM] * 5 + [HBM] * 8,
        out_specs=(VMEM, SMEM),
        scratch_shapes=[
            pltpu.VMEM((4,) + block, F32),
            pltpu.VMEM((2 * room,) + block, BF16),
            pltpu.VMEM((2 * room,) + block, BF16),
            pltpu.VMEM((2 * stored,) + block, BF16),
            pltpu.VMEM((2 * stored,) + block, BF16),
            pltpu.VMEM((stored + rows,) + block, F32),
            pltpu.VMEM((stored,) + block, F32),
            pltpu.SemaphoreType.DMA((4,)),
            pltpu.SemaphoreType.DMA((4,)),
        ],
        compiler_params=pltpu.CompilerParams(vmem_limit_bytes=VMEM_LIMIT),
        cost_estimate=pl.CostEstimate(
            flops=2**20, bytes_accessed=2**16, transcendentals=0
        ),
        name="first_halo",
    )(lists, left, right, offsets, weights, low, high, low_2, high_2, own_high, own_low, part, t)


def last_kernel(
    rows, slots, early, room_b,
    lists_ref, late_ref, left_ref, right_ref,
    low_ref, high_ref, own_high_ref, own_low_ref, given_ref,
    out_ref,
    got, far_high, far_low, own_high, own_low, held, got_sems, own_sems, in_sems, out_sems,
):
    plans = (left_ref, right_ref)
    sources = (low_ref, high_ref)
    sum_counts = [plans[side][SUM_ROW[side]] for side in range(2)]
    counts = [
        sum_counts[side] + jnp.maximum(plans[side][COUNT_ROW[side]] - early, 0) for side in range(2)
    ]
    own_count, out_count = late_ref[OF_COUNT, 0], late_ref[OF_COUNT, 1]

    def fetch(side, i):
        return pltpu.make_async_copy(sources[side].at[i], got.at[side, i], got_sems.at[side, i])

    def load(i):
        q = late_ref[OF_OUT, i]
        return pltpu.make_async_copy(given_ref.at[q], held.at[q], in_sems.at[q])

    def store(i):
        q = late_ref[OF_OUT, i]
        return pltpu.make_async_copy(held.at[q], out_ref.at[q], out_sems.at[q])

    def own_copies(i):
        at = late_ref[OF_OWN, i]
        return (
            pltpu.make_async_copy(own_high_ref.at[at], own_high.at[at], own_sems.at[0, at]),
            pltpu.make_async_copy(own_low_ref.at[at], own_low.at[at], own_sems.at[1, at]),
        )

    def start_own(i):
        for copy in own_copies(i):
            copy.start()

    def wait_own(i):
        for copy in own_copies(i):
            copy.wait()

    for side in range(2):
        over(counts[side], lambda i, side=side: fetch(side, i).start())
    over(own_count, start_own)
    over(out_count, lambda i: load(i).start())
    for side in range(2):
        over(counts[side], lambda i, side=side: fetch(side, i).wait())

        def convert(i):
            split_block(got.at[side], i, far_high, far_low, side * room_b + i)

        over(counts[side], convert, sum_counts[side])
    over(own_count, wait_own)

    def compute(i):
        q, low_at, high_at = late_ref[OF_OUT, i], late_ref[OF_LOW, i], late_ref[OF_HIGH, i]
        load(i).wait()
        for side, at in ((0, low_at), (1, high_at)):

            @pl.when(at >= 0)
            def _():
                def act(part):
                    held[q, part, :] -= 0.5 * got[side, at, part, :]

                stripes(held.shape[1:], act)

        def term(m):
            left = lists_ref[LAST, LEFT, m]
            right = lists_ref[LAST, RIGHT, m]
            add_product(held, q, -0.5, own_high, own_low, left, far_high, far_low, right)

        over(lists_ref[LAST, BEGIN, q + 1], term, lists_ref[LAST, BEGIN, q])
        store(i).start()

    over(out_count, compute)
    over(out_count, lambda i: store(i).wait())


def last_part(lists, late, left, right, low, high, own_high, own_low, given, early, rows, slots):
    room_b = low.shape[0]
    stored = rows * slots
    block = given.shape[1:]
    return pl.pallas_call(
        functools.partial(last_kernel, rows, slots, early, room_b),
        out_shape=jax.ShapeDtypeStruct(given.shape, F32),
        in_specs=[SMEM] * 4 + [HBM] * 5,
        out_specs=HBM,
        input_output_aliases={8: 0},
        scratch_shapes=[
            pltpu.VMEM((2, room_b) + block, F32),
            pltpu.VMEM((2 * room_b,) + block, BF16),
            pltpu.VMEM((2 * room_b,) + block, BF16),
            pltpu.VMEM((2 * stored,) + block, BF16),
            pltpu.VMEM((2 * stored,) + block, BF16),
            pltpu.VMEM((stored,) + block, F32),
            pltpu.SemaphoreType.DMA((2, room_b)),
            pltpu.SemaphoreType.DMA((2, 2 * stored)),
            pltpu.SemaphoreType.DMA((stored,)),
            pltpu.SemaphoreType.DMA((stored,)),
        ],
        compiler_params=pltpu.CompilerParams(vmem_limit_bytes=VMEM_LIMIT),
        cost_estimate=pl.CostEstimate(
            flops=2**20, bytes_accessed=2**16, transcendentals=0
        ),
        name="last_halo",
    )(lists, late, left, right, low, high, own_high, own_low, given)


def partners(value, n, step):
    return lax.ppermute(value, AXES, [(i, i ^ step) for i in range(n)])


def steps_of(n):
    step = 1
    while step < n:
        yield (step, 2 * step, 3 * step) if 2 * step < n else (step,)
        step *= 4


def gather_all(value, n):
    if n & (n - 1):
        return lax.all_gather(value, AXES)
    value = value[None]
    for steps in steps_of(n):
        value = jnp.concatenate([value] + [partners(value, n, step) for step in steps])
    me = lax.axis_index(AXES)
    step = 1
    while step < n:
        pairs = value.reshape((n // (2 * step), 2, step) + value.shape[1:])
        value = jnp.where((me // step) % 2 == 0, pairs, pairs[:, ::-1]).reshape(value.shape)
        step *= 2
    return value


def sum_steps(n):
    inner = lax.axis_size(AXES[1])
    steps = [2**i for i in range(n.bit_length() - 1)]
    return [step for step in steps if step >= inner] + [step for step in steps if step < inner]


def sum_over(value, n, steps):
    for step in steps:
        value = value + partners(value, n, step)
    return value


def body(density_blocks, density_live, tangent_blocks, tangent_live, block_offsets):
    rows, slots = density_live.shape
    block = density_blocks.shape[2:]
    n = lax.axis_size("row") * lax.axis_size("col")
    me = lax.axis_index(AXES).astype(I32)
    x = density_blocks.reshape((rows * slots,) + block)
    t = tangent_blocks.reshape((rows * slots,) + block)
    offsets = block_offsets.reshape(-1)
    weights = tangent_live.reshape(-1)

    meta = jnp.concatenate([density_live, tangent_live, block_offsets], axis=1)
    gathered = gather_all(meta, n)
    worst = len(need_cells(0))
    rooms = tuple(r for r in (15, 16, 17, 18, 19, 20, 22) if r < worst) + (worst,)
    plan = make_plan(gathered, me, slots, rooms)
    left, right = plan[:, 0], plan[:, 1]

    index = jnp.arange(rows * slots, dtype=I32).reshape(rows, slots, 1)
    here = block_offsets[:, :, None] == jnp.arange(-HALF, HALF + 1, dtype=I32)
    own = jnp.stack(
        [
            jnp.max(jnp.where(here & (live == 1)[:, :, None], index + shift, -1), axis=1)
            for live, shift in ((density_live, 0), (tangent_live, rows * slots))
        ]
    ).reshape(-1)

    forward = [(i, (i + 1) % n) for i in range(n)]
    backward = [(b, a) for a, b in forward]

    def exchange(forth, back):
        return lax.ppermute(forth, AXES, forward), lax.ppermute(back, AXES, backward)

    def with_room(room, own, left, right, offsets, weights, x, t):
        room_a, room_c, room_b = split_room(room)
        early = room_a + room_c
        forth, back, sent = pack(own, left, right, x, t, 0, room_a, rows)
        low, high = exchange(forth, back)
        forth, back, _ = pack(own, left, right, x, t, room_a, early, rows)
        low_2, high_2 = exchange(forth, back)
        own, _, _ = lax.optimization_barrier((own, forth, back))
        part, own_high, own_low, lists, _, late = own_part(
            own, left, right, offsets, x, t, room_a, room_c, room_b, rows, slots
        )
        forth, back, help_trace = help_part(
            sent, left, right, lists, low, high, own_high, own_low, x, t, early, room_b, rows
        )
        forth, back, low_2, high_2 = lax.optimization_barrier((forth, back, low_2, high_2))
        last_low, last_high = exchange(forth, back)
        given, trace = first_part(
            lists, left, right, offsets, weights, low, high, low_2, high_2, own_high, own_low, part, t, rows, slots
        )
        trace = trace + help_trace
        steps = [] if n & (n - 1) else sum_steps(n)
        trace = sum_over(trace, n, steps[:-1])
        last_low, last_high, trace = lax.optimization_barrier((last_low, last_high, trace))
        out = last_part(lists, late, left, right, last_low, last_high, own_high, own_low, given, early, rows, slots)
        trace = sum_over(trace, n, steps[-1:]) if steps else lax.psum(trace, AXES)
        return out, trace

    out, trace = lax.switch(
        left[CHOICE_ROW],
        [functools.partial(with_room, room) for room in rooms],
        own, left, right, offsets, weights, x, t,
    )
    mean_trace = trace[0, 0] / (rows * n)
    return out.reshape(tangent_blocks.shape), mean_trace


def solution(mesh):
    return jax.shard_map(
        body,
        mesh=mesh,
        in_specs=(
            P(AXES, None, None, None),
            P(AXES, None),
            P(AXES, None, None, None),
            P(AXES, None),
            P(AXES, None),
        ),
        out_specs=(P(AXES, None, None, None), P()),
        check_vma=False,
    )
```

```python
import functools

import jax
import jax.numpy as jnp
from jax import lax
from jax.experimental import pallas as pl
from jax.experimental.pallas import tpu as pltpu
from jax.sharding import PartitionSpec as P

HALF = 3
WIDTH = 2 * HALF + 1
WIN = 2 * HALF
AXES = ("row", "col")
VMEM_LIMIT = 58 * 1024 * 1024
F32 = jnp.float32
BF16 = jnp.bfloat16
I32 = jnp.int32


def need_cells(side):
    base = 0 if side == 0 else HALF
    return [
        (t, k, j)
        for t in range(2)
        for k in range(HALF)
        for j in range(WIN)
        if abs(j - (base + k)) <= HALF
    ]


def cell(t, k, j):
    return (t * HALF + k) * WIN + j


CELLS = 2 * HALF * WIN
RESULTS = HALF * WIN
CELL_ROW = (0, CELLS)
RESULT_ROW = (2 * CELLS, 2 * CELLS + RESULTS)
BIT_ROW = 2 * CELLS + 2 * RESULTS
COUNT_ROW = (BIT_ROW + WIN, BIT_ROW + WIN + 1)
LEFT_ROW = (BIT_ROW + WIN + 2, BIT_ROW + WIN + 3)
SUM_ROW = (BIT_ROW + WIN + 4, BIT_ROW + WIN + 5)
CHOICE_ROW = BIT_ROW + WIN + 6
PLAN_ROWS = 128


SECOND = 2


def split_room(room):
    last = room * 9 // 20
    return room - SECOND - last, SECOND, last


def room_for_sums(sums):
    return ((20 * sums + 8) * 57) >> 9


def room_for_early(blocks):
    return ((20 * (blocks - 1) * 373) >> 12) + 1


def either(flags):
    return functools.reduce(jnp.bitwise_or, flags)


def plan_kernel(slots, rooms, me_ref, meta_ref, out_ref, table):
    n = meta_ref.shape[-1]
    fields = 3 * slots

    def row(i, f):
        source, r = (0, i) if i < HALF else (1, i - HALF)
        at = r * fields + f
        return meta_ref[source, at : at + 1, :]

    one = jnp.ones((1, n), I32)
    zero = jnp.zeros((1, n), I32)
    live = [{}, {}]
    kept, shown = {}, {}
    for i in range(WIN):
        offs = [row(i, 2 * slots + s) for s in range(slots)]
        flags = [[jnp.where(row(i, t * slots + s) == 1, one, zero) for s in range(slots)] for t in range(2)]
        for j in range(WIN):
            d = j - i
            if abs(d) > HALF:
                continue
            here = [jnp.where(o == d, one, zero) for o in offs]
            kept[i, j] = either(here)
            shown[i, j] = one if d == 0 else kept[i, j]
            for t in range(2):
                live[t][i, j] = either([h & f for h, f in zip(here, flags[t])])

    def near(*pairs):
        return all(abs(p - q) <= HALF for p, q in pairs)

    as_left = {}
    for side in range(2):
        base, other = (0, HALF) if side == 0 else (HALF, 0)
        for t, k, j in need_cells(side):
            if other <= j < other + HALF:
                ends = [
                    live[1 - t][j, e] & shown[base + k, e] for e in range(WIN) if near((e, j), (e, base + k))
                ]
                as_left[side, t, k, j] = live[t][base + k, j] & either(ends)
    sums = {}
    for side in range(2):
        base, other = (0, HALF) if side == 0 else (HALF, 0)
        for i in range(other, other + HALF):
            for j in range(WIN):
                if near((i, j)):
                    terms = [
                        live[t][i, k] & live[1 - t][k, j]
                        for t in range(2)
                        for k in range(base, base + HALF)
                        if near((i, k), (k, j))
                    ]
                    if terms:
                        sums[side, i, j] = kept[i, j] & either(terms)

    def visit(bits, on_left, on_cell, on_sum):
        for side in range(2):
            base, other = (0, HALF) if side == 0 else (HALF, 0)

            def is_cross(spec):
                return other <= spec[2] < other + HALF

            lefts = {}
            for spec in need_cells(side):
                if is_cross(spec):
                    t, k, j = spec
                    lefts[spec] = bits[base + k] & as_left[side, t, k, j]
                    on_left(side, spec, lefts[spec])
            for spec in sorted(need_cells(side), key=lambda c: not is_cross(c)):
                t, k, j = spec
                kk = base + k
                users = [
                    live[1 - t][i, kk] & shown[i, j] & (1 - bits[i])
                    for i in range(other, other + HALF)
                    if near((i, kk), (i, j))
                ]
                need = either(users) & live[t][kk, j]
                if spec in lefts:
                    need = need & (1 - lefts[spec])
                on_cell(side, spec, is_cross(spec), need, lefts.get(spec))
            for i in range(other, other + HALF):
                for j in range(WIN):
                    if (side, i, j) in sums:
                        on_sum(side, i - other, j, sums[side, i, j] & bits[i])

    trials = 2**WIN
    trial = lax.broadcasted_iota(I32, (trials, n), 0)
    totals = {}

    def tally(name, side, value):
        totals[name, side] = totals[name, side] + value if (name, side) in totals else value

    def count_left(side, spec, need):
        for name in ("all", "cross", "left"):
            tally(name, side, need)

    def count_cell(side, spec, cross, need, left):
        tally("all", side, need)
        if cross:
            tally("cross", side, need)

    visit(
        [(trial >> i) & 1 for i in range(WIN)],
        count_left,
        count_cell,
        lambda side, i, j, need: tally("sum", side, need),
    )
    cost = jnp.zeros((trials, n), I32)
    load = jnp.zeros((trials, n), I32)
    for side in range(2):
        both = totals["all", side] + totals["sum", side]
        load = load + both
        cost = jnp.maximum(cost, both)
        cost = jnp.maximum(cost, room_for_early(totals["cross", side]))
        cost = jnp.maximum(cost, room_for_sums(totals["sum", side]))
        cost = jnp.maximum(cost, room_for_early(totals["left", side] + SECOND))
    score = ((cost * 256 + load) * trials + trial).astype(F32)
    best = jnp.min(score, axis=0, keepdims=True)
    best = best.astype(I32)
    bits = [(best >> i) & 1 for i in range(WIN)]
    top = jnp.max((best >> (8 + WIN)).astype(F32), axis=1, keepdims=True).astype(I32)

    table[...] = jnp.full(table.shape, -1, I32)

    def put(at, value):
        table[at : at + 1, :] = value

    counts = {key: zero for key in [(name, side) for name in ("all", "left", "sum") for side in range(2)]}

    left_places = {}

    def place_left(side, spec, need):
        left_places[side, spec] = jnp.where(need == 1, counts["all", side], -one)
        for name in ("all", "left"):
            counts[name, side] = counts[name, side] + need

    def place_cell(side, spec, cross, need, left):
        place = left_places.get((side, spec), -one)
        put(CELL_ROW[side] + cell(*spec), jnp.where(need == 1, counts["all", side], place))
        counts["all", side] = counts["all", side] + need

    def place_sum(side, i, j, need):
        put(RESULT_ROW[side] + i * WIN + j, jnp.where(need == 1, counts["sum", side], -one))
        counts["sum", side] = counts["sum", side] + need

    visit(bits, place_left, place_cell, place_sum)
    for i in range(WIN):
        put(BIT_ROW + i, bits[i])
    for side in range(2):
        put(COUNT_ROW[side], counts["all", side])
        put(LEFT_ROW[side], counts["left", side])
        put(SUM_ROW[side], counts["sum", side])
    choice = sum(jnp.where(top > room, 1, 0) for room in rooms[:-1])
    put(CHOICE_ROW, jnp.broadcast_to(choice, (1, n)))

    me = me_ref[0]
    whole = table[...]
    lane = lax.broadcasted_iota(I32, whole.shape, 1)
    right = lax.rem(me + 1, n)
    first = jnp.sum(jnp.where(lane == me, whole, 0), axis=1, keepdims=True)
    second = jnp.sum(jnp.where(lane == right, whole, 0), axis=1, keepdims=True)
    out_lane = lax.broadcasted_iota(I32, out_ref.shape, 1)
    out_ref[...] = jnp.where(out_lane == 0, first, second)


def make_plan(meta, me, slots, rooms):
    n, rows = meta.shape[0], meta.shape[1]
    low = jnp.roll(meta[:, rows - HALF :], 1, axis=0).reshape(n, -1).T
    high = meta[:, :HALF].reshape(n, -1).T
    return pl.pallas_call(
        functools.partial(plan_kernel, slots, rooms),
        out_shape=jax.ShapeDtypeStruct((PLAN_ROWS, 128), I32),
        in_specs=[pl.BlockSpec(memory_space=pltpu.SMEM), pl.BlockSpec(memory_space=pltpu.VMEM)],
        out_specs=pl.BlockSpec(memory_space=pltpu.VMEM),
        scratch_shapes=[pltpu.VMEM((PLAN_ROWS, n), I32)],
        name="plan",
    )(me.reshape(1), jnp.stack([low, high]))


SMEM = pl.BlockSpec(memory_space=pltpu.SMEM)
VMEM = pl.BlockSpec(memory_space=pltpu.VMEM)
HBM = pl.BlockSpec(memory_space=pl.ANY)
SENT = 2 * HALF * WIN + 1


def over(count, act, begin=0):
    def step(i, carry):
        act(i)
        return carry

    lax.fori_loop(begin, count, step, 0)


def list_sent(rows, own_ref, left_ref, right_ref, sent_ref):
    for side, plan_ref in ((0, right_ref), (1, left_ref)):
        for t, k, j in need_cells(side):
            own_row = rows - HALF + k if side == 0 else k
            place = j - k + HALF if side == 0 else j - k
            at = plan_ref[CELL_ROW[side] + cell(t, k, j)]
            at = jnp.where(at >= 0, at, SENT - 1)
            sent_ref[side * SENT + at] = own_ref[(t * rows + own_row) * WIDTH + place]


class Carrier:
    def __init__(self, side, low, high, shift, sent_ref, x_ref, t_ref, out, held, sems_in, sems_out):
        self.side, self.low, self.count, self.shift = side, low, jnp.maximum(high - low, 0), shift
        self.sent_ref, self.sources, self.out, self.held = sent_ref, (x_ref, t_ref), out, held
        self.sems_in, self.sems_out = sems_in, sems_out

    def arrival(self, t, block, i):
        return pltpu.make_async_copy(self.sources[t].at[block], self.held.at[self.side, i], self.sems_in.at[self.side, i])

    def departure(self, i):
        target = self.out.at[self.shift + i]
        return pltpu.make_async_copy(self.held.at[self.side, i], target, self.sems_out.at[self.side, i])

    def begin(self):
        stored = self.sources[0].shape[0]

        def act(i):
            block = self.sent_ref[self.side * SENT + self.low + i]
            for t in range(2):

                @pl.when((block >= stored) == (t == 1))
                def _():
                    self.arrival(t, block - t * stored, i).start()

        over(self.count, act)

    def onward(self):
        def act(i):
            self.arrival(0, 0, i).wait()
            self.departure(i).start()

        over(self.count, act)

    def end(self):
        over(self.count, lambda i: self.departure(i).wait())


def pack_kernel(rows, low, high, sides, own_ref, left_ref, right_ref, x_ref, t_ref, *refs):
    outs, (sent_ref, held, sems_in, sems_out) = refs[: len(sides)], refs[len(sides) :]
    list_sent(rows, own_ref, left_ref, right_ref, sent_ref)
    counts = (right_ref[COUNT_ROW[0]], left_ref[COUNT_ROW[1]])
    carriers = [
        Carrier(side, low, jnp.minimum(counts[side], high), 0, sent_ref, x_ref, t_ref, out, held, sems_in, sems_out)
        for side, out in zip(sides, outs)
    ]
    for carrier in carriers:
        carrier.begin()
    for carrier in carriers:
        carrier.onward()
    for carrier in carriers:
        carrier.end()


def pack(own, left, right, x, t, low, high, rows, sides):
    block = x.shape[1:]
    room = high - low
    shape = jax.ShapeDtypeStruct((room,) + block, F32)
    return pl.pallas_call(
        functools.partial(pack_kernel, rows, low, high, sides),
        out_shape=(shape,) * len(sides) + (jax.ShapeDtypeStruct((2 * SENT,), I32),),
        in_specs=[SMEM] * 3 + [HBM] * 2,
        out_specs=(HBM,) * len(sides) + (SMEM,),
        scratch_shapes=[
            pltpu.VMEM((2, room) + block, F32),
            pltpu.SemaphoreType.DMA((2, room)),
            pltpu.SemaphoreType.DMA((2, room)),
        ],
        compiler_params=pltpu.CompilerParams(vmem_limit_bytes=VMEM_LIMIT),
        name="pack",
    )(own, left, right, x, t)


def halves(values):
    high = values.astype(BF16)
    return high, (values - high.astype(F32)).astype(BF16)


STRIPE = 32


def stripes(block, act):
    over(block[0] // STRIPE, lambda i: act(pl.ds(pl.multiple_of(i * STRIPE, STRIPE), STRIPE)))


def split_block(source, at, high_ref, low_ref, to):
    def act(part):
        high_ref[to, part, :], low_ref[to, part, :] = halves(source[at, part, :])

    stripes(source.shape[1:], act)


def add_product(total, at, sign, lh, ll, i, rh, rl, j):
    dot = functools.partial(jnp.dot, preferred_element_type=F32)
    half = total.shape[-2] // 2

    def act(h):
        part = pl.ds(pl.multiple_of(h * half, half), half)
        high, low = lh[i, part, :], ll[i, part, :]
        result = dot(high, rh[j]) + (dot(high, rl[j]) + dot(low, rh[j]))
        total[at, part, :] += result if sign == 1 else sign * result

    over(2, act)


OWN, FIRST, LAST, HELP = range(4)
LEFT, RIGHT, BEGIN = range(3)
OF_OWN, OF_OUT, OF_LOW, OF_HIGH, OF_COUNT = range(5)


def list_length(rows, slots):
    return -(-((rows * slots + rows) * 2 * WIDTH + 1) // 128) * 128


def own_kernel(
    rows, slots, room_a, room_c, room_b,
    own_ref, left_ref, right_ref, off_ref, x_ref, t_ref,
    part_ref, high_ref, low_ref, lists_ref, used_ref, late_ref,
):
    stored = rows * slots
    outs = stored + rows
    early = room_a + room_c
    late = [left_ref[SUM_ROW[0]] - early, room_b + right_ref[SUM_ROW[1]] - early]

    def clear(i, carry):
        used_ref[i] = 0
        return carry

    lax.fori_loop(0, 2 * stored, clear, 0)

    def of_output(q, counts):
        is_diag = q >= stored
        row = jnp.where(is_diag, q - stored, lax.div(q, slots))
        d = jnp.where(is_diag, 0, off_ref[jnp.minimum(q, stored - 1)])
        has_zero = jnp.bool_(False)
        for s in range(slots):
            has_zero = has_zero | (off_ref[row * slots + s] == 0)
        wanted = jnp.logical_not(is_diag & has_zero)
        for which in (OWN, FIRST, LAST):
            lists_ref[which, BEGIN, q] = counts[which]
        low_row = row - (rows - HALF)
        left_open = (row < HALF) & (left_ref[BIT_ROW + HALF + jnp.minimum(row, HALF - 1)] == 0)
        right_open = (low_row >= 0) & (right_ref[BIT_ROW + jnp.maximum(low_row, 0)] == 0)
        column = row + d

        def of_term(m, counts):
            t = lax.rem(m, 2)
            e = lax.div(m, 2) - HALF
            k = row + e
            place = d - e + HALF
            ok = wanted & (place >= 0) & (place < WIDTH)
            left = own_ref[(t * rows + row) * WIDTH + e + HALF]
            ok = ok & (left >= 0)
            is_own = ok & (k >= 0) & (k < rows)
            is_low = ok & (k < 0) & left_open
            is_high = ok & (k >= rows) & right_open
            own_block = own_ref[jnp.where(is_own, ((1 - t) * rows + k) * WIDTH + place, 0)]
            low_at = ((1 - t) * HALF + k + HALF) * WIN + column + HALF
            low_block = left_ref[CELL_ROW[0] + jnp.where(is_low, low_at, 0)]
            high_at = ((1 - t) * HALF + k - rows) * WIN + column - rows + HALF
            high_block = right_ref[CELL_ROW[1] + jnp.where(is_high, high_at, 0)]
            far_block = jnp.where(is_low, low_block, high_block)
            far_ok = (is_low | is_high) & (far_block >= 0)
            own_count, first_count, last_count = counts
            lists_ref[OWN, LEFT, own_count] = left
            lists_ref[OWN, RIGHT, own_count] = own_block
            own_count = own_count + jnp.where(is_own & (own_block >= 0), 1, 0)
            lists_ref[FIRST, LEFT, first_count] = left
            lists_ref[FIRST, RIGHT, first_count] = far_block + jnp.where(is_low, 0, early)
            first_count = first_count + jnp.where(far_ok & (far_block < early), 1, 0)
            lists_ref[LAST, LEFT, last_count] = left
            lists_ref[LAST, RIGHT, last_count] = far_block + jnp.where(is_low, late[0], late[1])
            is_last = far_ok & (far_block >= early)
            last_count = last_count + jnp.where(is_last, 1, 0)

            @pl.when(is_last)
            def _():
                used_ref[left] = 1

            return own_count, first_count, last_count

        return lax.fori_loop(0, 2 * WIDTH, of_term, counts)

    ends = lax.fori_loop(0, outs, of_output, (jnp.int32(0),) * 3)
    for which in (OWN, FIRST, LAST):
        lists_ref[which, BEGIN, outs] = ends[which]

    def list_own(i, count):
        late_ref[OF_OWN, count] = i
        return count + used_ref[i]

    late_ref[OF_COUNT, 0] = lax.fori_loop(0, 2 * stored, list_own, jnp.int32(0))

    def list_out(q, count):
        row = lax.div(q, slots)
        column = row + off_ref[q]
        base = rows - HALF
        low_ok = (row < HALF) & (column < HALF)
        low_at = left_ref[RESULT_ROW[0] + jnp.where(low_ok, row * WIN + column + HALF, 0)]
        low_at = jnp.where(low_ok, low_at, -1)
        high_ok = (row >= base) & (column >= base)
        high_at = right_ref[RESULT_ROW[1] + jnp.where(high_ok, (row - base) * WIN + column - base, 0)]
        high_at = jnp.where(high_ok, high_at, -1)
        late_ref[OF_OUT, count] = q
        late_ref[OF_LOW, count] = low_at
        late_ref[OF_HIGH, count] = high_at
        more = lists_ref[LAST, BEGIN, q + 1] > lists_ref[LAST, BEGIN, q]
        return count + jnp.where((low_at >= 0) | (high_at >= 0) | more, 1, 0)

    late_ref[OF_COUNT, 1] = lax.fori_loop(0, stored, list_out, jnp.int32(0))

    count = jnp.int32(0)
    for side, plan_ref in ((0, right_ref), (1, left_ref)):
        base, other = (0, HALF) if side == 0 else (HALF, 0)
        shift = rows - HALF if side == 0 else 0

        def of_sum(q, count):
            i = lax.div(q, WIN)
            j = lax.rem(q, WIN)
            open_row = plan_ref[BIT_ROW + other + i] == 1
            shown = (plan_ref[RESULT_ROW[side] + q] >= 0) | (j == other + i)
            open_row = open_row & shown
            lists_ref[HELP, BEGIN, side * RESULTS + q] = count

            def of_term(m, count):
                t = lax.rem(m, 2)
                k = lax.div(m, 2)
                reach = j - (base + k)
                ok = open_row & (reach >= -HALF) & (reach <= HALF)
                across = other + i - (base + k)
                ok = ok & (across >= -HALF) & (across <= HALF)
                left = plan_ref[CELL_ROW[1 - side] + (t * HALF + i) * WIN + base + k]
                right_at = jnp.where(ok, ((1 - t) * rows + shift + k) * WIDTH + reach + HALF, 0)
                right = own_ref[right_at]
                lists_ref[HELP, LEFT, count] = left + (room_a if side == 0 else 0)
                lists_ref[HELP, RIGHT, count] = right
                return count + jnp.where(ok & (left >= 0) & (right >= 0), 1, 0)

            return lax.fori_loop(0, 2 * HALF, of_term, count)

        count = lax.fori_loop(0, RESULTS, of_sum, count)
    lists_ref[HELP, BEGIN, 2 * RESULTS] = count

    def split(i, carry):
        for t, source in enumerate((x_ref, t_ref)):
            split_block(source, i, high_ref, low_ref, t * stored + i)
        return carry

    lax.fori_loop(0, stored, split, 0)

    def compute(q, carry):
        part_ref[q] = jnp.zeros(part_ref.shape[1:], F32)

        def term(m, carry):
            left = lists_ref[OWN, LEFT, m]
            right = lists_ref[OWN, RIGHT, m]
            add_product(part_ref, q, 1, high_ref, low_ref, left, high_ref, low_ref, right)
            return carry

        return lax.fori_loop(lists_ref[OWN, BEGIN, q], lists_ref[OWN, BEGIN, q + 1], term, carry)

    lax.fori_loop(0, outs, compute, 0)


def own_part(own, left, right, offsets, x, t, room_a, room_c, room_b, rows, slots):
    stored = rows * slots
    block = x.shape[1:]
    length = list_length(rows, slots)
    return pl.pallas_call(
        functools.partial(own_kernel, rows, slots, room_a, room_c, room_b),
        out_shape=(
            jax.ShapeDtypeStruct((stored + rows,) + block, F32),
            jax.ShapeDtypeStruct((2 * stored,) + block, BF16),
            jax.ShapeDtypeStruct((2 * stored,) + block, BF16),
            jax.ShapeDtypeStruct((4, 3, length), I32),
            jax.ShapeDtypeStruct((2 * stored,), I32),
            jax.ShapeDtypeStruct((5, 128), I32),
        ),
        in_specs=[SMEM] * 4 + [VMEM] * 2,
        out_specs=(VMEM, VMEM, VMEM, SMEM, SMEM, SMEM),
        compiler_params=pltpu.CompilerParams(vmem_limit_bytes=VMEM_LIMIT),
        cost_estimate=pl.CostEstimate(
            flops=2**20, bytes_accessed=2**16, transcendentals=0
        ),
        name="own_rows",
    )(own, left, right, offsets, x, t)


def convert_blocks(source, count, shift, far_high, far_low, stage, stage_sems):
    depth = stage.shape[0]

    def fetch(i):
        slot = lax.rem(i, depth)
        return pltpu.make_async_copy(source.at[i], stage.at[slot], stage_sems.at[slot])

    for i in range(depth - 1):

        @pl.when(i < count)
        def _():
            fetch(i).start()

    def convert(i, carry):
        @pl.when(i + depth - 1 < count)
        def _():
            fetch(i + depth - 1).start()

        fetch(i).wait()
        split_block(stage, lax.rem(i, depth), far_high, far_low, shift + i)
        return carry

    lax.fori_loop(0, count, convert, 0)


def trace_of(ref, at):
    side = ref.shape[-1]

    def stripe(i, total):
        first = pl.multiple_of(i * STRIPE, STRIPE)
        row = lax.broadcasted_iota(I32, (STRIPE, side), 0) + first
        column = lax.broadcasted_iota(I32, (STRIPE, side), 1)
        return total + jnp.where(row == column, ref[at, pl.ds(first, STRIPE), :], 0.0)

    return jnp.sum(lax.fori_loop(0, side // STRIPE, stripe, jnp.zeros((STRIPE, side), F32)))


def help_kernel(
    rows, room_a, early, room_b,
    sent_ref, left_ref, right_ref, lists_ref,
    low_ref, high_ref, own_high_ref, own_low_ref, x_ref, t_ref,
    forth_out, back_out, trace_ref,
    stage, far_high, far_low, own_high, own_low, sums, held, stage_sems, sems, sum_sems, sems_in, sems_out,
):
    outs = (forth_out, back_out)
    copies = [
        pltpu.make_async_copy(source, target, sems.at[i])
        for i, (source, target) in enumerate(((own_high_ref, own_high), (own_low_ref, own_low)))
    ]
    helps = lists_ref[HELP, BEGIN, 2 * RESULTS] > 0

    @pl.when(helps)
    def _():
        for copy in copies:
            copy.start()

    shifts = (right_ref[SUM_ROW[0]], left_ref[SUM_ROW[1]])
    carriers = [
        Carrier(side, early, count, shifts[side], sent_ref, x_ref, t_ref, outs[side], held, sems_in, sems_out)
        for side, count in ((0, right_ref[COUNT_ROW[0]]), (1, left_ref[COUNT_ROW[1]]))
    ]
    for carrier in carriers:
        carrier.begin()
    trace_ref[0, 0] = jnp.float32(0)

    @pl.when(helps)
    def _():
        convert_blocks(low_ref, left_ref[LEFT_ROW[0]], 0, far_high, far_low, stage, stage_sems)
        convert_blocks(high_ref, right_ref[LEFT_ROW[1]], room_a, far_high, far_low, stage, stage_sems)
        for copy in copies:
            copy.wait()

    for carrier in carriers:
        carrier.onward()
    for side, plan_ref in ((0, right_ref), (1, left_ref)):
        other = HALF if side == 0 else 0

        def compute(q, carry):
            begin_at = lists_ref[HELP, BEGIN, side * RESULTS + q]
            end_at = lists_ref[HELP, BEGIN, side * RESULTS + q + 1]
            at = plan_ref[RESULT_ROW[side] + q]

            @pl.when(end_at > begin_at)
            def _():
                slot = jnp.where(at >= 0, at, room_b)
                sums[side, slot] = jnp.zeros(sums.shape[2:], F32)

                def term(m, carry):
                    left = lists_ref[HELP, LEFT, m]
                    right = lists_ref[HELP, RIGHT, m]
                    add_product(sums.at[side], slot, 1, far_high, far_low, left, own_high, own_low, right)
                    return carry

                lax.fori_loop(begin_at, end_at, term, 0)

                @pl.when(at >= 0)
                def _():
                    pltpu.make_async_copy(sums.at[side, slot], outs[side].at[slot], sum_sems.at[side, slot]).start()

                @pl.when(lax.rem(q, WIN) == other + lax.div(q, WIN))
                def _():
                    trace_ref[0, 0] += trace_of(sums.at[side], slot)

            return carry

        lax.fori_loop(0, RESULTS, compute, 0)
    for side in range(2):

        def finish(i, carry):
            pltpu.make_async_copy(sums.at[side, i], outs[side].at[i], sum_sems.at[side, i]).wait()
            return carry

        lax.fori_loop(0, shifts[side], finish, 0)
    for carrier in carriers:
        carrier.end()


def help_part(sent, left, right, lists, low, high, own_high, own_low, x, t, early, room_b, rows):
    room_a = low.shape[0]
    block = x.shape[1:]
    stored = x.shape[0]
    shape = jax.ShapeDtypeStruct((room_b,) + block, F32)
    return pl.pallas_call(
        functools.partial(help_kernel, rows, room_a, early, room_b),
        out_shape=(shape, shape, jax.ShapeDtypeStruct((1, 1), F32)),
        in_specs=[SMEM] * 4 + [HBM] * 6,
        out_specs=(HBM, HBM, SMEM),
        scratch_shapes=[
            pltpu.VMEM((4,) + block, F32),
            pltpu.VMEM((2 * room_a,) + block, BF16),
            pltpu.VMEM((2 * room_a,) + block, BF16),
            pltpu.VMEM((2 * stored,) + block, BF16),
            pltpu.VMEM((2 * stored,) + block, BF16),
            pltpu.VMEM((2, room_b + 1) + block, F32),
            pltpu.VMEM((2, room_b) + block, F32),
            pltpu.SemaphoreType.DMA((4,)),
            pltpu.SemaphoreType.DMA((2,)),
            pltpu.SemaphoreType.DMA((2, room_b)),
            pltpu.SemaphoreType.DMA((2, room_b)),
            pltpu.SemaphoreType.DMA((2, room_b)),
        ],
        compiler_params=pltpu.CompilerParams(vmem_limit_bytes=VMEM_LIMIT),
        cost_estimate=pl.CostEstimate(
            flops=2**20, bytes_accessed=2**16, transcendentals=0
        ),
        name="help_rows",
)(sent, left, right, lists, low, high, own_high, own_low, x, t)


def first_kernel(
    rows, slots, room_a, room_c,
    lists_ref, left_ref, right_ref, off_ref, weight_ref,
    low_ref, high_ref, low_ref_2, high_ref_2, own_high_ref, own_low_ref, part_ref, t_ref,
    out_ref, trace_ref,
    stage, far_high, far_low, own_high, own_low, total, tangent, stage_sems, sems,
):
    stored = rows * slots
    outs = stored + rows
    copies = [
        pltpu.make_async_copy(source, target, sems.at[i])
        for i, (source, target) in enumerate(
            ((own_high_ref, own_high), (own_low_ref, own_low), (part_ref, total), (t_ref, tangent))
        )
    ]
    for copy in copies:
        copy.start()
    early = room_a + room_c
    for side, (source, source_2, plan_ref) in enumerate(
        ((low_ref, low_ref_2, left_ref), (high_ref, high_ref_2, right_ref))
    ):
        whole = plan_ref[COUNT_ROW[side]]
        convert_blocks(source, jnp.minimum(whole, room_a), side * early, far_high, far_low, stage, stage_sems)
        count = jnp.maximum(jnp.minimum(whole, early) - room_a, 0)
        convert_blocks(source_2, count, side * early + room_a, far_high, far_low, stage, stage_sems)
    for copy in copies:
        copy.wait()

    trace_ref[0, 0] = jnp.float32(0)

    def compute(q, carry):
        def term(m, carry):
            left = lists_ref[FIRST, LEFT, m]
            right = lists_ref[FIRST, RIGHT, m]
            add_product(total, q, 1, own_high, own_low, left, far_high, far_low, right)
            return carry

        lax.fori_loop(lists_ref[FIRST, BEGIN, q], lists_ref[FIRST, BEGIN, q + 1], term, 0)

        @pl.when(q < stored)
        def _():
            at = jnp.minimum(q, stored - 1)
            scale = 1.5 * weight_ref[at].astype(F32)

            def act(part):
                out_ref[at, part, :] = scale * tangent[at, part, :] - 0.5 * total[q, part, :]

            stripes(total.shape[1:], act)

        @pl.when((q >= stored) | (off_ref[jnp.minimum(q, stored - 1)] == 0))
        def _():
            trace_ref[0, 0] += trace_of(total, q)

        return carry

    lax.fori_loop(0, outs, compute, 0)


def first_part(lists, left, right, offsets, weights, low, high, low_2, high_2, own_high, own_low, part, t, rows, slots):
    room_a, room_c = low.shape[0], low_2.shape[0]
    room = room_a + room_c
    stored = rows * slots
    block = t.shape[1:]
    return pl.pallas_call(
        functools.partial(first_kernel, rows, slots, room_a, room_c),
        out_shape=(
            jax.ShapeDtypeStruct((stored,) + block, F32),
            jax.ShapeDtypeStruct((1, 1), F32),
        ),
        in_specs=[SMEM] * 5 + [HBM] * 8,
        out_specs=(VMEM, SMEM),
        scratch_shapes=[
            pltpu.VMEM((4,) + block, F32),
            pltpu.VMEM((2 * room,) + block, BF16),
            pltpu.VMEM((2 * room,) + block, BF16),
            pltpu.VMEM((2 * stored,) + block, BF16),
            pltpu.VMEM((2 * stored,) + block, BF16),
            pltpu.VMEM((stored + rows,) + block, F32),
            pltpu.VMEM((stored,) + block, F32),
            pltpu.SemaphoreType.DMA((4,)),
            pltpu.SemaphoreType.DMA((4,)),
        ],
        compiler_params=pltpu.CompilerParams(vmem_limit_bytes=VMEM_LIMIT),
        cost_estimate=pl.CostEstimate(
            flops=2**20, bytes_accessed=2**16, transcendentals=0
        ),
        name="first_halo",
    )(lists, left, right, offsets, weights, low, high, low_2, high_2, own_high, own_low, part, t)


def last_kernel(
    rows, slots, early, room_b,
    lists_ref, late_ref, left_ref, right_ref,
    low_ref, high_ref, own_high_ref, own_low_ref, given_ref,
    out_ref,
    got, far_high, far_low, own_high, own_low, held, got_sems, own_sems, in_sems, out_sems,
):
    plans = (left_ref, right_ref)
    sources = (low_ref, high_ref)
    sum_counts = [plans[side][SUM_ROW[side]] for side in range(2)]
    counts = [
        sum_counts[side] + jnp.maximum(plans[side][COUNT_ROW[side]] - early, 0) for side in range(2)
    ]
    own_count, out_count = late_ref[OF_COUNT, 0], late_ref[OF_COUNT, 1]

    def fetch(side, i):
        return pltpu.make_async_copy(sources[side].at[i], got.at[side, i], got_sems.at[side, i])

    def load(i):
        q = late_ref[OF_OUT, i]
        return pltpu.make_async_copy(given_ref.at[q], held.at[q], in_sems.at[q])

    def store(i):
        q = late_ref[OF_OUT, i]
        return pltpu.make_async_copy(held.at[q], out_ref.at[q], out_sems.at[q])

    def own_copies(i):
        at = late_ref[OF_OWN, i]
        return (
            pltpu.make_async_copy(own_high_ref.at[at], own_high.at[at], own_sems.at[0, at]),
            pltpu.make_async_copy(own_low_ref.at[at], own_low.at[at], own_sems.at[1, at]),
        )

    def start_own(i):
        for copy in own_copies(i):
            copy.start()

    def wait_own(i):
        for copy in own_copies(i):
            copy.wait()

    for side in range(2):
        over(counts[side], lambda i, side=side: fetch(side, i).start())
    over(own_count, start_own)
    over(out_count, lambda i: load(i).start())
    for side in range(2):
        over(counts[side], lambda i, side=side: fetch(side, i).wait())

        def convert(i):
            split_block(got.at[side], i, far_high, far_low, side * room_b + i)

        over(counts[side], convert, sum_counts[side])
    over(own_count, wait_own)

    def compute(i):
        q, low_at, high_at = late_ref[OF_OUT, i], late_ref[OF_LOW, i], late_ref[OF_HIGH, i]
        load(i).wait()
        for side, at in ((0, low_at), (1, high_at)):

            @pl.when(at >= 0)
            def _():
                def act(part):
                    held[q, part, :] -= 0.5 * got[side, at, part, :]

                stripes(held.shape[1:], act)

        def term(m):
            left = lists_ref[LAST, LEFT, m]
            right = lists_ref[LAST, RIGHT, m]
            add_product(held, q, -0.5, own_high, own_low, left, far_high, far_low, right)

        over(lists_ref[LAST, BEGIN, q + 1], term, lists_ref[LAST, BEGIN, q])
        store(i).start()

    over(out_count, compute)
    over(out_count, lambda i: store(i).wait())


def last_part(lists, late, left, right, low, high, own_high, own_low, given, early, rows, slots):
    room_b = low.shape[0]
    stored = rows * slots
    block = given.shape[1:]
    return pl.pallas_call(
        functools.partial(last_kernel, rows, slots, early, room_b),
        out_shape=jax.ShapeDtypeStruct(given.shape, F32),
        in_specs=[SMEM] * 4 + [HBM] * 5,
        out_specs=HBM,
        input_output_aliases={8: 0},
        scratch_shapes=[
            pltpu.VMEM((2, room_b) + block, F32),
            pltpu.VMEM((2 * room_b,) + block, BF16),
            pltpu.VMEM((2 * room_b,) + block, BF16),
            pltpu.VMEM((2 * stored,) + block, BF16),
            pltpu.VMEM((2 * stored,) + block, BF16),
            pltpu.VMEM((stored,) + block, F32),
            pltpu.SemaphoreType.DMA((2, room_b)),
            pltpu.SemaphoreType.DMA((2, 2 * stored)),
            pltpu.SemaphoreType.DMA((stored,)),
            pltpu.SemaphoreType.DMA((stored,)),
        ],
        compiler_params=pltpu.CompilerParams(vmem_limit_bytes=VMEM_LIMIT),
        cost_estimate=pl.CostEstimate(
            flops=2**20, bytes_accessed=2**16, transcendentals=0
        ),
        name="last_halo",
    )(lists, late, left, right, low, high, own_high, own_low, given)


def partners(value, n, step):
    return lax.ppermute(value, AXES, [(i, i ^ step) for i in range(n)])


def steps_of(n):
    step = 1
    while step < n:
        yield (step, 2 * step, 3 * step) if 2 * step < n else (step,)
        step *= 4


def gather_all(value, n):
    if n & (n - 1):
        return lax.all_gather(value, AXES)
    value = value[None]
    for steps in steps_of(n):
        value = jnp.concatenate([value] + [partners(value, n, step) for step in steps])
    me = lax.axis_index(AXES)
    step = 1
    while step < n:
        pairs = value.reshape((n // (2 * step), 2, step) + value.shape[1:])
        value = jnp.where((me // step) % 2 == 0, pairs, pairs[:, ::-1]).reshape(value.shape)
        step *= 2
    return value


def sum_steps(n):
    inner = lax.axis_size(AXES[1])
    steps = [2**i for i in range(n.bit_length() - 1)]
    return [step for step in steps if step >= inner] + [step for step in steps if step < inner]


def sum_over(value, n, steps):
    for step in steps:
        value = value + partners(value, n, step)
    return value


def body(density_blocks, density_live, tangent_blocks, tangent_live, block_offsets):
    rows, slots = density_live.shape
    block = density_blocks.shape[2:]
    n = lax.axis_size("row") * lax.axis_size("col")
    me = lax.axis_index(AXES).astype(I32)
    x = density_blocks.reshape((rows * slots,) + block)
    t = tangent_blocks.reshape((rows * slots,) + block)
    offsets = block_offsets.reshape(-1)
    weights = tangent_live.reshape(-1)

    meta = jnp.concatenate([density_live, tangent_live, block_offsets], axis=1)
    gathered = gather_all(meta, n)
    worst = len(need_cells(0))
    rooms = tuple(r for r in (15, 16, 17, 18, 19, 20, 22) if r < worst) + (worst,)
    plan = make_plan(gathered, me, slots, rooms)
    left, right = plan[:, 0], plan[:, 1]

    index = jnp.arange(rows * slots, dtype=I32).reshape(rows, slots, 1)
    here = block_offsets[:, :, None] == jnp.arange(-HALF, HALF + 1, dtype=I32)
    own = jnp.stack(
        [
            jnp.max(jnp.where(here & (live == 1)[:, :, None], index + shift, -1), axis=1)
            for live, shift in ((density_live, 0), (tangent_live, rows * slots))
        ]
    ).reshape(-1)

    forward = [(i, (i + 1) % n) for i in range(n)]
    backward = [(b, a) for a, b in forward]

    def exchange(forth, back):
        return lax.ppermute(forth, AXES, forward), lax.ppermute(back, AXES, backward)

    def with_room(room, own, left, right, offsets, weights, x, t):
        room_a, room_c, room_b = split_room(room)
        early = room_a + room_c
        forth, sent = pack(own, left, right, x, t, 0, room_a, rows, (0,))
        back, _ = pack(own, left, right, x, t, 0, room_a, rows, (1,))
        low, high = exchange(forth, back)
        forth, back, _ = pack(own, left, right, x, t, room_a, early, rows, (0, 1))
        low_2, high_2 = exchange(forth, back)
        own, _, _ = lax.optimization_barrier((own, forth, back))
        part, own_high, own_low, lists, _, late = own_part(
            own, left, right, offsets, x, t, room_a, room_c, room_b, rows, slots
        )
        forth, back, help_trace = help_part(
            sent, left, right, lists, low, high, own_high, own_low, x, t, early, room_b, rows
        )
        forth, back, low_2, high_2 = lax.optimization_barrier((forth, back, low_2, high_2))
        last_low, last_high = exchange(forth, back)
        given, trace = first_part(
            lists, left, right, offsets, weights, low, high, low_2, high_2, own_high, own_low, part, t, rows, slots
        )
        trace = trace + help_trace
        steps = [] if n & (n - 1) else sum_steps(n)
        trace = sum_over(trace, n, steps[:-1])
        last_low, last_high, trace = lax.optimization_barrier((last_low, last_high, trace))
        out = last_part(lists, late, left, right, last_low, last_high, own_high, own_low, given, early, rows, slots)
        trace = sum_over(trace, n, steps[-1:]) if steps else lax.psum(trace, AXES)
        return out, trace

    out, trace = lax.switch(
        left[CHOICE_ROW],
        [functools.partial(with_room, room) for room in rooms],
        own, left, right, offsets, weights, x, t,
    )
    mean_trace = trace[0, 0] / (rows * n)
    return out.reshape(tangent_blocks.shape), mean_trace


def solution(mesh):
    return jax.shard_map(
        body,
        mesh=mesh,
        in_specs=(
            P(AXES, None, None, None),
            P(AXES, None),
            P(AXES, None, None, None),
            P(AXES, None),
            P(AXES, None),
        ),
        out_specs=(P(AXES, None, None, None), P()),
        check_vma=False,
    )
```
